512 devices in a mesh: feat: 32 (over y, z_hi, core), layer: 4 (over x), dp: 4 (over z_lo).
Axes of the slice: x: 4, y: 4, z: 16 (z_hi: 4, z_lo: 4; z = z_hi * 4 + z_lo), core: 2. Of those that a mesh axis runs over, the one named last changes fastest.
Arguments:
- residual: bfloat16 [4, 1024, 2304], P('layer', 'dp'), may hold values from -6 to 6
- enc_weight: bfloat16 [4, 2304, 8192], P('layer', None, 'feat'), may hold values from -0.125 to 0.125
- enc_bias: float32 [4, 8192], P('layer', 'feat'), may hold values from -0.6 to 0.3
- dec_weight: bfloat16 [4, 4, 8192, 2304], P(None, 'layer', 'feat', 'dp'), may hold values from -0.046875 to 0.046875
- dec_bias: float32 [4, 2304], P('layer', 'dp'), may hold values from -3 to 3
- target: bfloat16 [4, 1024, 2304], P('layer', 'feat', 'dp'), may hold values from -6 to 6
Outputs:
- enc_grad: bfloat16 [4, 2304, 8192], P('layer', 'dp', 'feat')
- dec_grad: bfloat16 [4, 4, 8192, 2304], P(None, 'layer', 'feat', 'dp')
The draws below stay inside these ranges and needn't reach their ends.
All inputs are finite; a program needn't handle non-finite values.
Results may differ from the reference program's by a relative error of at most 0.023.
Values may be sent and summed in bfloat16 or wider, within the bound.
A program may use at most 64 MiB of HBM per device.

```python
import math
import jax
import jax.numpy as jnp
from jax import lax

D = 2304
FEAT = 8192
TOK_DEV = 256
LAYERS = 4
TOKENS = 1024
COLS = 576
N_DP = 4


def steps_of(rng, dims, cuts, least, top_value):
    def one(dim, shards_of):
        draws = jax.random.uniform(jax.random.fold_in(jax.random.fold_in(rng, 6), dim), (shards_of,), jnp.float32, least / len(cuts), top_value / len(cuts))
        return jnp.repeat(jnp.exp(draws), dims[dim] // shards_of).reshape((-1,) + (1,) * (len(dims) - dim - 1))

    level = one(*cuts[0])
    for cut in cuts[1:]:
        level = level * one(*cut)
    return level


def noise(stream_key, dims, spread, bound, shards=(), kind=jnp.bfloat16):
    factor_of = steps_of(stream_key, dims, shards, -0.22, 0.18) if shards else 1.0
    entries = jax.random.normal(stream_key, dims, jnp.float32) * spread * factor_of
    return jnp.minimum(jnp.maximum(entries, -bound), bound).astype(kind)


def setup_inputs(seed: int = 0) -> dict:
    key_list = jax.random.split(jax.random.key(seed), 7)
    return {
        "residual": noise(key_list[0], (LAYERS, TOKENS, D), 1.0, 6.0, ((0, 4), (1, 4))),
        "enc_weight": noise(key_list[1], (LAYERS, D, FEAT), D ** -0.5, 0.125, ((0, 4), (2, 32))),
        "enc_bias": jnp.clip(-0.6 + 0.90000004 * jax.random.uniform(key_list[2], (LAYERS, FEAT), jnp.float32) ** steps_of(key_list[2], (LAYERS, FEAT), ((0, 4), (1, 32)), -0.2, 0.2), -0.6, 0.3),
        "dec_weight": noise(key_list[3], (LAYERS, LAYERS, FEAT, D), (2 * FEAT) ** -0.5, 0.046875, ((1, 4), (2, 32), (3, 4))),
        "dec_bias": noise(key_list[4], (LAYERS, D), 0.5, 3.0, ((0, 4), (1, 4)), jnp.float32),
        "target": noise(key_list[5], (LAYERS, TOKENS, D), 1.0, 6.0, ((0, 4), (1, 32), (2, 4))),
    }


def reference(residual, enc_weight, enc_bias, dec_weight, dec_bias, target):
    loss_scale = 1.0 / math.sqrt(TOKENS)
    pre_acts = []
    code_list = []
    for src_layer in range(LAYERS):
        pre_act = jnp.dot(residual[src_layer], enc_weight[src_layer], preferred_element_type=jnp.float32) + enc_bias[src_layer].astype(jnp.float32)
        positive = jnp.maximum(pre_act, 0.0)
        pre_acts.append(pre_act)
        code_list.append((positive * positive).astype(jnp.bfloat16))
    error_grads = []
    for dst_layer in range(LAYERS):
        recon = dec_bias[dst_layer].astype(jnp.float32)[None, :]
        for src_layer in range(dst_layer + 1):
            recon = recon + jnp.dot(code_list[src_layer], dec_weight[src_layer, dst_layer], preferred_element_type=jnp.float32)
        error_grads.append(((recon - target[dst_layer].astype(jnp.float32)) * loss_scale).astype(jnp.bfloat16))
    dec_rows = []
    for src_layer in range(LAYERS):
        row_blocks = []
        for dst_layer in range(LAYERS):
            if src_layer <= dst_layer:
                row_blocks.append(jnp.dot(code_list[src_layer].T, error_grads[dst_layer], preferred_element_type=jnp.float32).astype(jnp.bfloat16))
            else:
                row_blocks.append(jnp.zeros((FEAT, D), jnp.bfloat16))
        dec_rows.append(jnp.stack(row_blocks))
    dec_grad = jnp.stack(dec_rows)
    enc_list = []
    for src_layer in range(LAYERS):
        running = jnp.zeros((TOKENS, FEAT), jnp.float32)
        for dst_layer in range(src_layer, LAYERS):
            for block_idx in range(N_DP):
                first_col = block_idx * COLS
                partial_value = jnp.dot(error_grads[dst_layer][:, first_col:first_col + COLS], dec_weight[src_layer, dst_layer][:, first_col:first_col + COLS].T, preferred_element_type=jnp.float32).astype(jnp.bfloat16)
                running = running + lax.optimization_barrier(partial_value).astype(jnp.float32)
        code_grad = (running * 2.0 * jnp.maximum(pre_acts[src_layer], 0.0)).astype(jnp.bfloat16)
        enc_sum = jnp.zeros((D, FEAT), jnp.float32)
        for block_idx in range(N_DP):
            first_row = block_idx * TOK_DEV
            partial_value = jnp.dot(residual[src_layer][first_row:first_row + TOK_DEV].T, code_grad[first_row:first_row + TOK_DEV], preferred_element_type=jnp.float32).astype(jnp.bfloat16)
            enc_sum = enc_sum + lax.optimization_barrier(partial_value).astype(jnp.float32)
        enc_list.append(enc_sum.astype(jnp.bfloat16))
    enc_grad = jnp.stack(enc_list)
    return (enc_grad, dec_grad)
```

```python
import math

import jax
import jax.numpy as jnp
from jax import lax
from jax.experimental import pallas as pl
from jax.experimental.pallas import tpu as pltpu
from jax.sharding import PartitionSpec as P

MESH = pl.DeviceIdType.MESH
BF = jnp.bfloat16
F32 = jnp.float32
WIN = 640

SEMS = dict(
    load=3, ar=16, a_right=4, a_left=4, a_n1=4, a_n2=4, a_rl=4,
    rr=4, rr_s=4, rc=3, rc_s=3,
    pc=4, pc_s=4,
    yb=24, yb_s=24, zb=6, zb_s=6,
    cz=4, cz_s=4, cy=16, cy_s=16, cc=16, cc_s=16,
    xr=4, xl=4, xe=4, x_s=12, zc=8, zc_s=4, e=4, e_right=4, e_left=4,
)

SCRATCH = dict(
    resid=((256, 2304), BF), w=((2304, 256), BF), wt=((4, 576, 256), BF),
    pos=((256, 256), F32), codes=((16, 256, 256), BF),
    rw=((4, 256, WIN), BF), rwt=((4, WIN, 256), BF),
    acc=((4, 4, 2, 32, 576), F32), po=((4, 4, 32, 576), BF), pc=((4, 4, 32, 576), BF),
    yst=((24, 16, 576), BF), yb=((24, 16, 576), BF),
    tz=((4, 32, 576), F32), zst=((6, 16, 576), BF), zb=((6, 16, 576), BF),
    g=((4, 4, 2, 32, 576), BF), gt=((4, 576, 256), BF),
    bt=((16, 256, 256), BF), xr=((4, 256, 256), BF), xl=((4, 256, 256), BF), xe=((4, 256, 256), BF),
    s=((4, 256, 256), F32), ss=((4, 256, 256), BF), zc=((8, 256, 256), BF),
    cg=((4, 256, 256), BF), eacc=((WIN, 256), F32),
)


def body(*refs):
    resid_h, w_h, bias, wt_h, dbias, target, enc_o, dec_o = refs[:8]
    R = dict(zip(SCRATCH, refs[8 : 8 + len(SCRATCH)]))
    S = dict(zip(SEMS, refs[8 + len(SCRATCH) :]))
    resid, w, wt, pos, codes = R["resid"], R["w"], R["wt"], R["pos"], R["codes"]
    f = lax.axis_index("feat")
    t = lax.axis_index("layer")
    d = lax.axis_index("dp")
    c, z, y = lax.rem(f, 2), lax.rem(f // 2, 4), f // 8

    def at(yy, zz, core):
        return (lax.rem(yy + 8, 4) * 4 + lax.rem(zz + 8, 4)) * 2 + core

    def along_z(k):
        g = lax.rem(z * 4 + d + k + 16, 16)
        return (at(y, g // 4, c), t, lax.rem(g, 4))

    dev_core = (at(y, z, 1 - c), t, d)
    dev_yp, dev_ym = (at(y + 1, z, c), t, d), (at(y - 1, z, c), t, d)
    dev_zp, dev_zm = (at(y, z + 1, c), t, d), (at(y, z - 1, c), t, d)
    dev_xp, dev_xm = (f, lax.rem(t + 1, 4), d), (f, lax.rem(t + 3, 4), d)
    dev_r, dev_l = (f, t, lax.rem(d + 1, 4)), (f, t, lax.rem(d + 3, 4))

    def copy(src, dst, ssem, rsem, dev):
        return pltpu.make_async_remote_copy(
            src_ref=src, dst_ref=dst, send_sem=ssem, recv_sem=rsem, device_id=dev, device_id_type=MESH
        )

    def arrived(dst, rsem):
        copy(dst, dst, S["load"].at[0], rsem, dev_core).wait_recv()

    def sent(src, ssem):
        copy(src, src, ssem, S["load"].at[0], dev_core).wait_send()

    loads = [
        pltpu.make_async_copy(resid_h.at[0], resid, S["load"].at[0]),
        pltpu.make_async_copy(w_h.at[0], w, S["load"].at[1]),
        pltpu.make_async_copy(wt_h, wt, S["load"].at[2]),
    ]
    for one in loads:
        one.start()

    barrier = pltpu.get_barrier_semaphore()
    partners = [dev_core, dev_yp, dev_ym, dev_zp, dev_zm, dev_xp, dev_xm]
    partners += [along_z(k) for k in (1, -1, 2, -2)]
    for dev in partners:
        pl.semaphore_signal(barrier, inc=1, device_id=dev, device_id_type=MESH)
    pl.semaphore_wait(barrier, len(partners))

    loads[0].wait()
    loads[1].wait()
    pre = jnp.dot(resid[...], w[...], preferred_element_type=F32) + bias[...]
    positive = jnp.maximum(pre, 0.0)
    pos[...] = positive
    codes[t * 4 + d] = (positive * positive).astype(BF)

    def offset(i):
        half = (i + 1) // 2
        return jnp.where(lax.rem(i, 2) == 1, -half, half)

    def relays(b):
        return ((t == 0) & (b < 2)) | ((t == 2) & (b >= 2)) | (t == 3)

    relay_from = jnp.where(t == 3, 0, 1)
    dev_relay = (f, jnp.where(t == 3, 2, 3), d)

    def second(b):
        return (t == 0) | ((t == 1) & (b < 2))

    @pl.loop(0, 10)
    def _(i):
        b = d + offset(i)

        @pl.when((i < 7) & (b >= 0) & (b < 4))
        def _():
            blk = codes.at[t * 4 + b]
            sem = S["ar"].at[t * 4 + b]

            @pl.when(i > 0)
            def _():
                arrived(blk, sem)

            @pl.when((b <= d) & (d < 3))
            def _():
                copy(blk, blk, S["a_right"].at[b], sem, dev_r).start()

            @pl.when((b >= d) & (d > 0))
            def _():
                copy(blk, blk, S["a_left"].at[b], sem, dev_l).start()

            @pl.when(t < 3)
            def _():
                copy(blk, blk, S["a_n1"].at[b], sem, dev_xp).start()

            @pl.when(second(b))
            def _():
                copy(blk, blk, S["a_n2"].at[b], sem, dev_xm).start()

        rb = d + offset(jnp.maximum(i - 3, 0))

        @pl.when((i >= 3) & (rb >= 0) & (rb < 4))
        def _():
            @pl.when(relays(rb))
            def _():
                blk = codes.at[relay_from * 4 + rb]
                sem = S["ar"].at[relay_from * 4 + rb]
                arrived(blk, sem)
                copy(blk, blk, S["a_rl"].at[rb], sem, dev_relay).start()

    def start_col(k):
        return pl.multiple_of(k * 576 - 64 * lax.rem(k, 2), 128)

    rw = R["rw"]

    def move_cols(k, lo, size, slot):
        rows = pl.ds(pl.multiple_of(c * 128 + lo, 64), size)
        dev = along_z(k)
        src = resid.at[rows, pl.ds(start_col(dev[2]), WIN)]
        return copy(src, rw.at[d, rows], S["rr_s"].at[slot], S["rr"].at[slot], dev)

    col_moves = [move_cols(1, 0, 128, 0), move_cols(-1, 0, 128, 1), move_cols(2, 0, 64, 2), move_cols(-2, 64, 64, 3)]
    for one in col_moves:
        one.start()
    rw[d] = resid[:, pl.ds(start_col(d), WIN)]

    @pl.loop(0, 12)
    def _(i):
        l, b = i // 4, lax.rem(i, 4)
        relayed = relays(b) & (l == relay_from)

        @pl.when((l < t) & jnp.logical_not(relayed))
        def _():
            arrived(codes.at[i], S["ar"].at[i])

    loads[2].wait()

    acc, po, pc = R["acc"], R["po"], R["pc"]

    @pl.loop(0, 4)
    def _(b):
        for top in range(4):
            @pl.when(t == top)
            def _():
                total = None
                for l in range(top + 1):
                    term = lax.dot_general(
                        codes[l * 4 + b], wt[l], (((1,), (1,)), ((), ())), preferred_element_type=F32
                    )
                    total = term if total is None else total + term
                acc[b] = total.reshape(4, 2, 32, 576)

        po[b] = acc[b, :, 1 - c].astype(BF)
        copy(po.at[b], pc.at[b], S["pc_s"].at[b], S["pc"].at[b], dev_core).start()

    half = pl.ds(pl.multiple_of(c * 128, 128), 128)
    slots = [lax.rem(d + 3, 4), lax.rem(d + 1, 4), lax.rem(d + 2, 4)]
    first_half = pl.ds(pl.multiple_of(c * 128, 64), 64)
    last_half = pl.ds(pl.multiple_of(c * 128 + 64, 64), 64)
    arrived(rw.at[slots[0], half], S["rr"].at[0])
    arrived(rw.at[slots[1], half], S["rr"].at[1])
    arrived(rw.at[slots[2], first_half], S["rr"].at[2])
    arrived(rw.at[slots[2], last_half], S["rr"].at[3])
    core_moves = [
        copy(rw.at[k, half], rw.at[k, half], S["rc_s"].at[n], S["rc"].at[n], dev_core) for n, k in enumerate(slots)
    ]
    for one in core_moves:
        one.start()

    @pl.loop(0, 4)
    def _(b):
        arrived(pc.at[b], S["pc"].at[b])

    yst, yb = R["yst"], R["yb"]

    def chunk_z(i):
        return lax.rem(z + jnp.where(i == 0, 2, jnp.where(i == 1, 1, jnp.where(i == 2, 3, 0))), 4)

    def partial(yy, zz, h):
        rows = pl.ds(16 * h, 16)
        yy = lax.rem(yy + 4, 4)
        return acc[yy, zz, c, rows] + pc[yy, zz, rows].astype(F32)

    def y_send(i, k, value, dev):
        n = i * 6 + k
        yst[n] = value.astype(BF)
        copy(yst.at[n], yb.at[n], S["yb_s"].at[n], S["yb"].at[n], dev).start()

    def y_take(i, k):
        n = i * 6 + k
        arrived(yb.at[n], S["yb"].at[n])
        return yb[n].astype(F32)

    @pl.loop(0, 4)
    def _(i):
        zz = chunk_z(i)
        y_send(i, 0, partial(y + 2, zz, 0), dev_yp)
        y_send(i, 1, partial(y + 2, zz, 1), dev_ym)
        y_send(i, 2, partial(y + 1, zz, 1), dev_yp)
        y_send(i, 3, partial(y - 1, zz, 0), dev_ym)

    @pl.loop(0, 4)
    def _(i):
        zz = chunk_z(i)
        y_send(i, 4, partial(y + 1, zz, 0) + y_take(i, 0), dev_yp)
        y_send(i, 5, partial(y - 1, zz, 1) + y_take(i, 1), dev_ym)

    tz, zst, zb = R["tz"], R["zst"], R["zb"]

    def z_send(k, value, dev):
        zst[k] = value.astype(BF)
        copy(zst.at[k], zb.at[k], S["zb_s"].at[k], S["zb"].at[k], dev).start()

    def z_take(k):
        arrived(zb.at[k], S["zb"].at[k])
        return zb[k].astype(F32)

    @pl.loop(0, 4)
    def _(i):
        zz = chunk_z(i)
        top_half = partial(y, zz, 0) + y_take(i, 3) + y_take(i, 4)
        low_half = partial(y, zz, 1) + y_take(i, 2) + y_take(i, 5)
        tz[i, pl.ds(0, 16)] = top_half
        tz[i, pl.ds(16, 16)] = low_half

        @pl.when(i == 0)
        def _():
            z_send(0, top_half, dev_zp)
            z_send(1, low_half, dev_zm)

        @pl.when(i == 1)
        def _():
            z_send(2, low_half, dev_zp)

        @pl.when(i == 2)
        def _():
            z_send(3, top_half, dev_zm)

    z_send(4, tz[1, pl.ds(0, 16)] + z_take(0), dev_zp)
    z_send(5, tz[2, pl.ds(16, 16)] + z_take(1), dev_zm)
    scale = 1.0 / math.sqrt(1024)
    g = R["g"]
    for h, ks in enumerate(((3, 4), (2, 5))):
        rows = pl.ds(16 * h, 16)
        recon = tz[3, rows] + z_take(ks[0]) + z_take(ks[1])
        err = recon + dbias[...] - target[0, rows].astype(F32)
        g[y, z, c, rows] = (err * scale).astype(BF)

    up, down = pl.ds(0, 16), pl.ds(16, 16)

    def block_z(j):
        return lax.rem(z + jnp.where(j == 0, 0, jnp.where(j == 1, 3, jnp.where(j == 2, 1, 2))), 4)

    def to_core(yy, zz):
        n = yy * 4 + zz
        blk = g.at[yy, zz, c]
        copy(blk, blk, S["cc_s"].at[n], S["cc"].at[n], dev_core).start()

    def to_y(j):
        blk = g.at[y, block_z(j), c]
        copy(blk, blk, S["cy_s"].at[j * 4], S["cy"].at[j * 4], dev_yp).start()
        copy(blk, blk, S["cy_s"].at[j * 4 + 1], S["cy"].at[j * 4 + 1], dev_ym).start()
        to_core(y, block_z(j))

    ym, yp, y2 = lax.rem(y + 3, 4), lax.rem(y + 1, 4), lax.rem(y + 2, 4)
    zm, zp, z2 = lax.rem(z + 3, 4), lax.rem(z + 1, 4), lax.rem(z + 2, 4)

    own = g.at[y, z, c]
    copy(own, own, S["cz_s"].at[0], S["cz"].at[0], dev_zp).start()
    copy(own, own, S["cz_s"].at[1], S["cz"].at[1], dev_zm).start()
    to_y(0)
    arrived(g.at[y, zm, c], S["cz"].at[0])
    part = g.at[y, zm, c, up]
    copy(part, part, S["cz_s"].at[2], S["cz"].at[2], dev_zp).start()
    to_y(1)
    arrived(g.at[y, zp, c], S["cz"].at[1])
    part = g.at[y, zp, c, down]
    copy(part, part, S["cz_s"].at[3], S["cz"].at[3], dev_zm).start()
    to_y(2)

    def y_forward(j):
        zz = block_z(j)
        arrived(g.at[ym, zz, c], S["cy"].at[j * 4])
        part = g.at[ym, zz, c, up]
        copy(part, part, S["cy_s"].at[j * 4 + 2], S["cy"].at[j * 4 + 2], dev_yp).start()
        to_core(ym, zz)
        arrived(g.at[yp, zz, c], S["cy"].at[j * 4 + 1])
        part = g.at[yp, zz, c, down]
        copy(part, part, S["cy_s"].at[j * 4 + 3], S["cy"].at[j * 4 + 3], dev_ym).start()
        to_core(yp, zz)

    y_forward(0)
    arrived(g.at[y, z2, c, up], S["cz"].at[2])
    arrived(g.at[y, z2, c, down], S["cz"].at[3])
    to_y(3)

    @pl.loop(1, 4)
    def _(j):
        y_forward(j)

    @pl.loop(0, 4)
    def _(j):
        zz = block_z(j)
        arrived(g.at[y2, zz, c, up], S["cy"].at[j * 4 + 2])
        arrived(g.at[y2, zz, c, down], S["cy"].at[j * 4 + 3])
        to_core(y2, zz)

    @pl.loop(0, 16)
    def _(n):
        arrived(g.at[n // 4, lax.rem(n, 4), 1 - c], S["cc"].at[n])

    bt, xr, xl, xe, s, ss, zc = R["bt"], R["xr"], R["xl"], R["xe"], R["s"], R["ss"], R["zc"]
    gt = R["gt"]

    def order(i):
        return jnp.where(i == 0, 0, jnp.where(i == 1, 3, i - 1))

    def x_send(k, b, l, dst, name, dev):
        copy(bt.at[l * 4 + b], dst.at[b], S["x_s"].at[k * 4 + b], S[name].at[b], dev).start()

    @pl.loop(0, 4)
    def _(i):
        b = order(i)
        for l in (1, 2, 0, 3):
            @pl.when(t >= l)
            def _():
                bt[l * 4 + b] = jnp.dot(
                    g[b].reshape(256, 576), wt[l], preferred_element_type=F32
                ).astype(BF)

        @pl.when(t == 1)
        def _():
            x_send(0, b, 0, xr, "xr", dev_xm)

        @pl.when(t == 2)
        def _():
            x_send(0, b, 0, xl, "xl", dev_xp)

            @pl.when(b < 2)
            def _():
                x_send(1, b, 1, xr, "xr", dev_xm)

        @pl.when(t == 3)
        def _():
            @pl.when(b < 2)
            def _():
                x_send(1, b, 1, xe, "xe", dev_xp)

            @pl.when(b >= 2)
            def _():
                x_send(1, b, 1, xe, "xe", dev_xm)

            x_send(2, b, 2, xr, "xr", dev_xm)

    @pl.loop(0, 4)
    def _(b):
        gt[b] = g[b].reshape(256, 576).T

    def add_in(l, b, other, name):
        arrived(other.at[b], S[name].at[b])
        bt[l * 4 + b] = (bt[l * 4 + b].astype(F32) + other[b].astype(F32)).astype(BF)

    @pl.loop(0, 5)
    def _(i):
        b = order(i)

        @pl.when(i < 4)
        def _():
            @pl.when(t == 3)
            def _():
                add_in(0, b, xl, "xl")
                x_send(0, b, 0, xl, "xl", dev_xp)

            @pl.when((t == 2) & (b >= 2))
            def _():
                add_in(1, b, xe, "xe")
                x_send(1, b, 1, xr, "xr", dev_xm)

            @pl.when((t == 0) & (b < 2))
            def _():
                arrived(xe.at[b], S["xe"].at[b])
                copy(xe.at[b], xl.at[b], S["x_s"].at[b], S["xl"].at[b], dev_xp).start()

            @pl.when(i <= t)
            def _():
                total = None
                for k in range(4):
                    term = jnp.dot(gt[k], codes[i * 4 + k], preferred_element_type=F32)
                    total = term if total is None else total + term
                dec_o[i] = total.astype(BF)

            @pl.when(i > t)
            def _():
                dec_o[i] = jnp.zeros((576, 256), BF)

        @pl.when(i > 0)
        def _():
            q = order(jnp.maximum(i - 1, 0))
            s[q] = bt[t * 4 + q].astype(F32)

            @pl.when(t < 3)
            def _():
                arrived(xr.at[q], S["xr"].at[q])
                s[q] += xr[q].astype(F32)

            @pl.when((t == 0) | ((t == 1) & (q < 2)))
            def _():
                arrived(xl.at[q], S["xl"].at[q])
                s[q] += xl[q].astype(F32)

            @pl.when((d < q) & (d > 0))
            def _():
                arrived(zc.at[q], S["zc"].at[q])
                s[q] += zc[q].astype(F32)

            @pl.when((d > q) & (d < 3))
            def _():
                arrived(zc.at[4 + q], S["zc"].at[4 + q])
                s[q] += zc[4 + q].astype(F32)

            @pl.when(d < q)
            def _():
                ss[q] = s[q].astype(BF)
                copy(ss.at[q], zc.at[q], S["zc_s"].at[q], S["zc"].at[q], dev_r).start()

            @pl.when(d > q)
            def _():
                ss[q] = s[q].astype(BF)
                copy(ss.at[q], zc.at[4 + q], S["zc_s"].at[q], S["zc"].at[4 + q], dev_l).start()

    rwt = R["rwt"]
    for n, k in enumerate(slots):
        other_half = pl.ds(pl.multiple_of((1 - c) * 128, 128), 128)
        arrived(rw.at[k, other_half], S["rc"].at[n])

    @pl.loop(0, 4)
    def _(k):
        rwt[k] = rw[k].T

    @pl.when(d > 0)
    def _():
        arrived(zc.at[d], S["zc"].at[d])
        s[d] += zc[d].astype(F32)

    @pl.when(d < 3)
    def _():
        arrived(zc.at[4 + d], S["zc"].at[4 + d])
        s[d] += zc[4 + d].astype(F32)

    cg, eacc = R["cg"], R["eacc"]
    cg[d] = (s[d] * 2.0 * pos[...]).astype(BF)

    eacc[...] = jnp.zeros_like(eacc)

    @pl.loop(0, 7)
    def _(i):
        b = d + offset(i)

        @pl.when((b >= 0) & (b < 4))
        def _():
            blk, sem = cg.at[b], S["e"].at[b]

            @pl.when(i > 0)
            def _():
                arrived(blk, sem)

            @pl.when((b <= d) & (d < 3))
            def _():
                copy(blk, blk, S["e_right"].at[b], sem, dev_r).start()

            @pl.when((b >= d) & (d > 0))
            def _():
                copy(blk, blk, S["e_left"].at[b], sem, dev_l).start()

            eacc[...] += jnp.dot(rwt[b], cg[b], preferred_element_type=F32)

    shift = pl.multiple_of(64 * lax.rem(d, 2), 64)
    enc_o[0] = eacc[pl.ds(shift, 576)].astype(BF)

    @pl.loop(0, 4)
    def _(b):
        blk = codes.at[b]

        @pl.when((b <= d) & (d < 3))
        def _():
            sent(blk, S["a_right"].at[b])
            sent(blk, S["e_right"].at[b])

        @pl.when((b >= d) & (d > 0))
        def _():
            sent(blk, S["a_left"].at[b])
            sent(blk, S["e_left"].at[b])

        @pl.when(t < 3)
        def _():
            sent(blk, S["a_n1"].at[b])

        @pl.when(second(b))
        def _():
            sent(blk, S["a_n2"].at[b])

        @pl.when(relays(b))
        def _():
            sent(blk, S["a_rl"].at[b])

        sent(po.at[b], S["pc_s"].at[b])

        @pl.when((t > 0) | (b < 2))
        def _():
            sent(blk, S["x_s"].at[b])

        @pl.when(t >= 2)
        def _():
            sent(blk, S["x_s"].at[4 + b])

        @pl.when(t == 3)
        def _():
            sent(blk, S["x_s"].at[8 + b])

        @pl.when(d != b)
        def _():
            sent(blk, S["zc_s"].at[b])

        sent(own, S["cy_s"].at[b * 4])
        sent(own, S["cy_s"].at[b * 4 + 1])
        sent(g.at[y, z, c, up], S["cy_s"].at[b * 4 + 2])
        sent(g.at[y, z, c, up], S["cy_s"].at[b * 4 + 3])

    @pl.loop(0, 24)
    def _(n):
        sent(yst.at[n], S["yb_s"].at[n])

    @pl.loop(0, 6)
    def _(n):
        sent(zst.at[n], S["zb_s"].at[n])

    @pl.loop(0, 16)
    def _(n):
        sent(own, S["cc_s"].at[n])

    sent(own, S["cz_s"].at[0])
    sent(own, S["cz_s"].at[1])
    sent(g.at[y, z, c, up], S["cz_s"].at[2])
    sent(g.at[y, z, c, up], S["cz_s"].at[3])
    for one in col_moves:
        one.wait_send()
    for one in core_moves:
        one.wait_send()


def shards(residual, enc_weight, enc_bias, dec_weight, dec_bias, target):
    wt = jnp.swapaxes(dec_weight[:, 0], 1, 2)
    vmem = pl.BlockSpec(memory_space=pltpu.VMEM)
    hbm = pl.BlockSpec(memory_space=pl.ANY)
    enc, dec = pl.pallas_call(
        body,
        out_shape=(
            jax.ShapeDtypeStruct((1, 576, 256), BF),
            jax.ShapeDtypeStruct((4, 576, 256), BF),
        ),
        in_specs=[hbm, hbm, vmem, hbm, vmem, vmem],
        out_specs=(vmem, vmem),
        scratch_shapes=[pltpu.VMEM(*spec) for spec in SCRATCH.values()]
        + [pltpu.SemaphoreType.DMA((n,)) for n in SEMS.values()],
        compiler_params=pltpu.CompilerParams(
            collective_id=0, has_side_effects=True, vmem_limit_bytes=56 * 1024 * 1024
        ),
    )(residual, enc_weight, enc_bias, wt, dec_bias, target)
    return enc, jnp.swapaxes(dec, 1, 2)[:, None]


def solution(mesh):
    in_specs = (
        P("layer", "dp", None),
        P("layer", None, "feat"),
        P("layer", "feat"),
        P(None, "layer", "feat", "dp"),
        P("layer", "dp"),
        P("layer", "feat", "dp"),
    )
    out_specs = (P("layer", "dp", "feat"), P(None, "layer", "feat", "dp"))
    return jax.shard_map(shards, mesh=mesh, in_specs=in_specs, out_specs=out_specs, check_vma=False)
```

```python
import math

import jax
import jax.numpy as jnp
from jax import lax
from jax.experimental import pallas as pl
from jax.experimental.pallas import tpu as pltpu
from jax.sharding import PartitionSpec as P

MESH = pl.DeviceIdType.MESH
BF = jnp.bfloat16
F32 = jnp.float32
WIN = 640
LAG = 5
WAVES = LAG + 7

SEMS = dict(
    load=3, ar=64, a_right=16, a_left=16, a_n1=16, a_n2=16, a_rl=16,
    rr=4, rr_s=4, rc=3, rc_s=3,
    pc=4, pc_s=4,
    yb=24, yb_s=24, zb=6, zb_s=6,
    cz=4, cz_s=4, cy=16, cy_s=16, cc=16, cc_s=16,
    xr=8, xl=8, xe=8, x_s=24, zc=32, zc_s=16, e=16, e_right=16, e_left=16,
)

SCRATCH = dict(
    resid=((256, 2304), BF), w=((2304, 256), BF), wt=((4, 576, 256), BF),
    pos=((4, 64, 256), F32), codes=((4, 4, 4, 64, 256), BF),
    rw=((4, 256, WIN), BF), rwt=((4, WIN, 256), BF),
    acc=((4, 4, 2, 32, 576), F32), po=((4, 4, 32, 576), BF), pc=((4, 4, 32, 576), BF),
    yst=((24, 16, 576), BF), yb=((24, 16, 576), BF),
    tz=((4, 32, 576), F32), zst=((6, 16, 576), BF), zb=((6, 16, 576), BF),
    g=((4, 4, 2, 32, 576), BF), gt=((4, 576, 256), BF),
    bt=((4, 4, 4, 64, 256), BF), xr=((8, 2, 64, 256), BF), xl=((8, 2, 64, 256), BF), xe=((8, 2, 64, 256), BF),
    s=((8, 2, 64, 256), F32), ss=((16, 64, 256), BF), zc=((32, 64, 256), BF),
    cg=((4, 4, 64, 256), BF), eacc=((WIN, 256), F32),
)


def order(p):
    return jnp.where(p == 0, 0, jnp.where(p == 1, 3, p - 1))


def place(b):
    return jnp.where(b == 0, 0, jnp.where(b == 3, 1, b + 1))


def body(*refs):
    resid_h, w_h, bias, wt_h, dbias, target, enc_o, dec_o = refs[:8]
    R = dict(zip(SCRATCH, refs[8 : 8 + len(SCRATCH)]))
    S = dict(zip(SEMS, refs[8 + len(SCRATCH) :]))
    resid, w, wt, pos, codes = R["resid"], R["w"], R["wt"], R["pos"], R["codes"]
    f = lax.axis_index("feat")
    t = lax.axis_index("layer")
    d = lax.axis_index("dp")
    c, z, y = lax.rem(f, 2), lax.rem(f // 2, 4), f // 8

    def at(yy, zz, core):
        return (lax.rem(yy + 8, 4) * 4 + lax.rem(zz + 8, 4)) * 2 + core

    def along_z(k):
        g = lax.rem(z * 4 + d + k + 16, 16)
        return (at(y, g // 4, c), t, lax.rem(g, 4))

    dev_core = (at(y, z, 1 - c), t, d)
    dev_yp, dev_ym = (at(y + 1, z, c), t, d), (at(y - 1, z, c), t, d)
    dev_zp, dev_zm = (at(y, z + 1, c), t, d), (at(y, z - 1, c), t, d)
    dev_xp, dev_xm = (f, lax.rem(t + 1, 4), d), (f, lax.rem(t + 3, 4), d)
    dev_r, dev_l = (f, t, lax.rem(d + 1, 4)), (f, t, lax.rem(d + 3, 4))
    ym, yp, y2 = lax.rem(y + 3, 4), lax.rem(y + 1, 4), lax.rem(y + 2, 4)
    zm, zp, z2 = lax.rem(z + 3, 4), lax.rem(z + 1, 4), lax.rem(z + 2, 4)
    pd = place(d)

    def copy(src, dst, ssem, rsem, dev):
        return pltpu.make_async_remote_copy(
            src_ref=src, dst_ref=dst, send_sem=ssem, recv_sem=rsem, device_id=dev, device_id_type=MESH
        )

    def arrived(dst, rsem):
        copy(dst, dst, S["load"].at[0], rsem, dev_core).wait_recv()

    def sent(src, ssem):
        copy(src, src, ssem, S["load"].at[0], dev_core).wait_send()

    loads = [
        pltpu.make_async_copy(resid_h.at[0], resid, S["load"].at[0]),
        pltpu.make_async_copy(w_h.at[0], w, S["load"].at[1]),
        pltpu.make_async_copy(wt_h, wt, S["load"].at[2]),
    ]
    for one in loads:
        one.start()

    barrier = pltpu.get_barrier_semaphore()
    partners = [dev_core, dev_yp, dev_ym, dev_zp, dev_zm, dev_xp, dev_xm]
    partners += [along_z(k) for k in (1, -1, 2, -2)]
    for dev in partners:
        pl.semaphore_signal(barrier, inc=1, device_id=dev, device_id_type=MESH)
    pl.semaphore_wait(barrier, len(partners))

    loads[0].wait()
    loads[1].wait()
    pre = jnp.dot(resid[...], w[...], preferred_element_type=F32) + bias[...]
    positive = jnp.maximum(pre, 0.0)
    pos[...] = positive.reshape(4, 64, 256)
    codes[t, :, pd] = (positive * positive).astype(BF).reshape(4, 64, 256)
    loads[2].wait()

    def chunk_z(i):
        return lax.rem(z + jnp.where(i == 0, 2, jnp.where(i == 1, 1, jnp.where(i == 2, 3, 0))), 4)

    def relays(b):
        side = (b == 0) | (b == 3)
        return ((t == 0) & side) | ((t == 2) & jnp.logical_not(side)) | (t == 3)

    relay_from = jnp.where(t == 3, 0, 1)
    dev_relay = (f, jnp.where(t == 3, 2, 3), d)

    def second(b):
        return (t == 0) | ((t == 1) & ((b == 0) | (b == 3)))

    def spread(i, b, fresh):
        p = place(b)
        n = i * 4 + p
        blk = codes.at[t, chunk_z(i), p]
        sem = S["ar"].at[t * 16 + n]

        if not fresh:
            arrived(blk, sem)

        @pl.when((b <= d) & (d < 3))
        def _():
            copy(blk, blk, S["a_right"].at[n], sem, dev_r).start()

        @pl.when((b >= d) & (d > 0))
        def _():
            copy(blk, blk, S["a_left"].at[n], sem, dev_l).start()

        @pl.when(t < 3)
        def _():
            copy(blk, blk, S["a_n1"].at[n], sem, dev_xp).start()

        @pl.when(second(b))
        def _():
            copy(blk, blk, S["a_n2"].at[n], sem, dev_xm).start()

    def relay(i, b):
        @pl.when(relays(b))
        def _():
            p = place(b)
            blk = codes.at[relay_from, chunk_z(i), p]
            sem = S["ar"].at[relay_from * 16 + i * 4 + p]
            arrived(blk, sem)
            copy(blk, blk, S["a_rl"].at[i * 4 + p], sem, dev_relay).start()

    rw, rwt = R["rw"], R["rwt"]

    def start_col(k):
        return pl.multiple_of(k * 576 - 64 * lax.rem(k, 2), 128)

    def move_cols(k, lo, size, slot):
        rows = pl.ds(pl.multiple_of(c * 128 + lo, 64), size)
        dev = along_z(k)
        src = resid.at[rows, pl.ds(start_col(dev[2]), WIN)]
        return copy(src, rw.at[pd, rows], S["rr_s"].at[slot], S["rr"].at[slot], dev)

    col_moves = [move_cols(1, 0, 128, 0), move_cols(-1, 0, 128, 1), move_cols(2, 0, 64, 2), move_cols(-2, 64, 64, 3)]
    half = pl.ds(pl.multiple_of(c * 128, 128), 128)
    other_half = pl.ds(pl.multiple_of((1 - c) * 128, 128), 128)
    slots = [place(lax.rem(d + k, 4)) for k in (3, 1, 2)]
    core_moves = [
        copy(rw.at[k, half], rw.at[k, half], S["rc_s"].at[n], S["rc"].at[n], dev_core) for n, k in enumerate(slots)
    ]

    acc, po, pc = R["acc"], R["po"], R["pc"]

    def recon_chunk(i):
        zz = chunk_z(i)

        @pl.loop(0, 12)
        def _(n):
            l, p = n // 4, lax.rem(n, 4)
            relayed = relays(order(p)) & (l == relay_from)

            @pl.when((l < t) & jnp.logical_not(relayed))
            def _():
                arrived(codes.at[l, zz, p], S["ar"].at[l * 16 + i * 4 + p])

        for top in range(4):
            @pl.when(t == top)
            def _():
                total = None
                for l in range(top + 1):
                    term = lax.dot_general(
                        codes[l, zz].reshape(256, 256), wt[l], (((1,), (1,)), ((), ())), preferred_element_type=F32
                    )
                    total = term if total is None else total + term
                acc[i] = total.reshape(4, 2, 32, 576)

        po[i] = acc[i, :, 1 - c].astype(BF)
        copy(po.at[i], pc.at[i], S["pc_s"].at[i], S["pc"].at[i], dev_core).start()

    yst, yb = R["yst"], R["yb"]

    def partial(i, yy, h):
        rows = pl.ds(16 * h, 16)
        p = place(yy)
        return acc[i, p, c, rows] + pc[i, p, rows].astype(F32)

    def y_send(i, k, value, dev):
        n = i * 6 + k
        yst[n] = value.astype(BF)
        copy(yst.at[n], yb.at[n], S["yb_s"].at[n], S["yb"].at[n], dev).start()

    def y_take(i, k):
        n = i * 6 + k
        arrived(yb.at[n], S["yb"].at[n])
        return yb[n].astype(F32)

    def y_first(i):
        arrived(pc.at[i], S["pc"].at[i])
        y_send(i, 0, partial(i, y2, 0), dev_yp)
        y_send(i, 1, partial(i, y2, 1), dev_ym)
        y_send(i, 2, partial(i, yp, 1), dev_yp)
        y_send(i, 3, partial(i, ym, 0), dev_ym)

    def y_second(i):
        y_send(i, 4, partial(i, yp, 0) + y_take(i, 0), dev_yp)
        y_send(i, 5, partial(i, ym, 1) + y_take(i, 1), dev_ym)

    tz, zst, zb = R["tz"], R["zst"], R["zb"]

    def z_send(k, value, dev):
        zst[k] = value.astype(BF)
        copy(zst.at[k], zb.at[k], S["zb_s"].at[k], S["zb"].at[k], dev).start()

    def z_take(k):
        arrived(zb.at[k], S["zb"].at[k])
        return zb[k].astype(F32)

    def z_first(i):
        top_half = partial(i, y, 0) + y_take(i, 3) + y_take(i, 4)
        low_half = partial(i, y, 1) + y_take(i, 2) + y_take(i, 5)
        tz[i, pl.ds(0, 16)] = top_half
        tz[i, pl.ds(16, 16)] = low_half

        @pl.when(i == 0)
        def _():
            z_send(0, top_half, dev_zp)
            z_send(1, low_half, dev_zm)

        @pl.when(i == 1)
        def _():
            z_send(2, low_half, dev_zp)

        @pl.when(i == 2)
        def _():
            z_send(3, top_half, dev_zm)
            z_send(4, tz[1, pl.ds(0, 16)] + z_take(0), dev_zp)
            z_send(5, tz[2, pl.ds(16, 16)] + z_take(1), dev_zm)

    @pl.loop(0, 4)
    def _(i):
        spread(i, d, True)

    @pl.loop(1, WAVES)
    def _(k):
        @pl.loop(0, 4)
        def _(i):
            h = k - i

            @pl.when((h > 0) & (h < 4))
            def _():
                for b in (d - h, d + h):
                    @pl.when((b >= 0) & (b < 4))
                    def _():
                        spread(i, b, False)

            m = k - 1 - i

            @pl.when((m >= 0) & (m < 4))
            def _():
                @pl.when(d >= m)
                def _():
                    relay(i, d - m)

                @pl.when((m > 0) & (d + m < 4))
                def _():
                    relay(i, d + m)

        @pl.when(k == 6)
        def _():
            for one in col_moves:
                one.start()
            rw[pd] = resid[:, pl.ds(start_col(d), WIN)]

        for lag, step in ((LAG, recon_chunk), (LAG + 1, y_first), (LAG + 2, y_second), (LAG + 3, z_first)):
            @pl.when((k >= lag) & (k < lag + 4))
            def _():
                step(k - lag)

        @pl.when(k == LAG + 3)
        def _():
            arrived(rw.at[slots[0], half], S["rr"].at[0])
            arrived(rw.at[slots[1], half], S["rr"].at[1])
            arrived(rw.at[slots[2], pl.ds(pl.multiple_of(c * 128, 64), 64)], S["rr"].at[2])
            arrived(rw.at[slots[2], pl.ds(pl.multiple_of(c * 128 + 64, 64), 64)], S["rr"].at[3])
            for one in core_moves:
                one.start()

    scale = 1.0 / math.sqrt(1024)
    g = R["g"]
    py = place(y)
    for h, ks in enumerate(((3, 4), (2, 5))):
        rows = pl.ds(16 * h, 16)
        recon = tz[3, rows] + z_take(ks[0]) + z_take(ks[1])
        err = recon + dbias[...] - target[0, rows].astype(F32)
        g[z, py, c, rows] = (err * scale).astype(BF)

    up, down = pl.ds(0, 16), pl.ds(16, 16)

    def block_z(j):
        return lax.rem(z + jnp.where(j == 0, 0, jnp.where(j == 1, 3, jnp.where(j == 2, 1, 2))), 4)

    def to_core(yy, j):
        n = j * 4 + place(yy)
        blk = g.at[block_z(j), place(yy), c]
        copy(blk, blk, S["cc_s"].at[n], S["cc"].at[n], dev_core).start()

    def to_y(j):
        blk = g.at[block_z(j), py, c]
        copy(blk, blk, S["cy_s"].at[j * 4], S["cy"].at[j * 4], dev_yp).start()
        copy(blk, blk, S["cy_s"].at[j * 4 + 1], S["cy"].at[j * 4 + 1], dev_ym).start()
        to_core(y, j)

    def y_forward(j):
        blk = g.at[block_z(j), place(ym), c]
        arrived(blk, S["cy"].at[j * 4])
        part = g.at[block_z(j), place(ym), c, up]
        copy(part, part, S["cy_s"].at[j * 4 + 2], S["cy"].at[j * 4 + 2], dev_yp).start()
        to_core(ym, j)
        blk = g.at[block_z(j), place(yp), c]
        arrived(blk, S["cy"].at[j * 4 + 1])
        part = g.at[block_z(j), place(yp), c, down]
        copy(part, part, S["cy_s"].at[j * 4 + 3], S["cy"].at[j * 4 + 3], dev_ym).start()
        to_core(yp, j)

    def y_last(j):
        arrived(g.at[block_z(j), place(y2), c, up], S["cy"].at[j * 4 + 2])
        arrived(g.at[block_z(j), place(y2), c, down], S["cy"].at[j * 4 + 3])
        to_core(y2, j)

    bt, xr, xl, xe, s, ss, zc = R["bt"], R["xr"], R["xl"], R["xe"], R["s"], R["ss"], R["zc"]
    gt, cg, eacc = R["gt"], R["cg"], R["eacc"]

    def x_send(k, u, l, dst, name, dev):
        src = bt.at[l, u // 2, pl.ds(2 * lax.rem(u, 2), 2)]
        copy(src, dst.at[u], S["x_s"].at[k * 8 + u], S[name].at[u], dev).start()

    def back(j):
        zz = block_z(j)

        @pl.loop(0, 4)
        def _(p):
            arrived(g.at[zz, p, 1 - c], S["cc"].at[j * 4 + p])

        @pl.loop(0, t + 1)
        def _(l):
            term = jnp.dot(g[zz].reshape(256, 576), wt[l], preferred_element_type=F32)
            bt[l, j] = term.astype(BF).reshape(4, 64, 256)

        for h in range(2):
            u = j * 2 + h

            @pl.when(t == 1)
            def _():
                x_send(0, u, 0, xr, "xr", dev_xm)

            @pl.when(t == 2)
            def _():
                x_send(0, u, 0, xl, "xl", dev_xp)
                if h == 0:
                    x_send(1, u, 1, xr, "xr", dev_xm)

            @pl.when(t == 3)
            def _():
                x_send(1, u, 1, xe, "xe", dev_xp if h == 0 else dev_xm)
                x_send(2, u, 2, xr, "xr", dev_xm)

    def add_in(l, u, other, name):
        arrived(other.at[u], S[name].at[u])
        j, part = u // 2, pl.ds(2 * lax.rem(u, 2), 2)
        bt[l, j, part] = (bt[l, j, part].astype(F32) + other[u].astype(F32)).astype(BF)

    def x_second(u):
        h = lax.rem(u, 2)

        @pl.when(t == 3)
        def _():
            add_in(0, u, xl, "xl")
            x_send(0, u, 0, xl, "xl", dev_xp)

        @pl.when((t == 2) & (h == 1))
        def _():
            add_in(1, u, xe, "xe")
            x_send(1, u, 1, xr, "xr", dev_xm)

        @pl.when((t == 0) & (h == 0))
        def _():
            arrived(xe.at[u], S["xe"].at[u])
            copy(xe.at[u], xl.at[u], S["x_s"].at[u], S["xl"].at[u], dev_xp).start()

    def chain(u, pos_in_line):
        @pl.loop(0, 2)
        def _(r):
            p = 2 * lax.rem(u, 2) + r
            n = (u // 2) * 4 + p
            q = order(p)
            rightward = (d == pos_in_line) & (q > pos_in_line)
            leftward = (d == 3 - pos_in_line) & (q < 3 - pos_in_line)
            for going, base, dev in ((rightward, 0, dev_r), (leftward, 16, dev_l)):
                @pl.when(going)
                def _():
                    value = s[u, r]
                    if pos_in_line > 0:
                        arrived(zc.at[base + n], S["zc"].at[base + n])
                        value = value + zc[base + n].astype(F32)
                    ss[n] = value.astype(BF)
                    copy(ss.at[n], zc.at[base + n], S["zc_s"].at[n], S["zc"].at[base + n], dev).start()

    def x_sum(u):
        h = lax.rem(u, 2)
        s[u] = bt[t, u // 2, pl.ds(2 * h, 2)].astype(F32)

        @pl.when(t < 3)
        def _():
            arrived(xr.at[u], S["xr"].at[u])
            s[u] += xr[u].astype(F32)

        @pl.when((t == 0) | ((t == 1) & (h == 0)))
        def _():
            arrived(xl.at[u], S["xl"].at[u])
            s[u] += xl[u].astype(F32)

        chain(u, 0)

    def final(u):
        @pl.when(pd // 2 == lax.rem(u, 2))
        def _():
            r = lax.rem(pd, 2)
            j = u // 2
            n = j * 4 + pd

            @pl.when(d > 0)
            def _():
                arrived(zc.at[n], S["zc"].at[n])
                s[u, r] += zc[n].astype(F32)

            @pl.when(d < 3)
            def _():
                arrived(zc.at[16 + n], S["zc"].at[16 + n])
                s[u, r] += zc[16 + n].astype(F32)

            cg[j, pd] = (s[u, r] * 2.0 * pos[block_z(j)]).astype(BF)
            blk, sem = cg.at[j, pd], S["e"].at[n]

            @pl.when(d < 3)
            def _():
                copy(blk, blk, S["e_right"].at[n], sem, dev_r).start()

            @pl.when(d > 0)
            def _():
                copy(blk, blk, S["e_left"].at[n], sem, dev_l).start()

    def gather(u, hops):
        @pl.loop(0, 2)
        def _(r):
            p = 2 * lax.rem(u, 2) + r
            n = (u // 2) * 4 + p
            q = order(p)
            blk, sem = cg.at[u // 2, p], S["e"].at[n]

            @pl.when((q == d - hops) | (q == d + hops))
            def _():
                arrived(blk, sem)

            @pl.when((q == d - hops) & (d < 3))
            def _():
                copy(blk, blk, S["e_right"].at[n], sem, dev_r).start()

            @pl.when((q == d + hops) & (d > 0))
            def _():
                copy(blk, blk, S["e_left"].at[n], sem, dev_l).start()

    def dec_grad(i):
        @pl.when(i <= t)
        def _():
            total = None
            for k in range(4):
                term = jnp.dot(gt[k], codes[i, k].reshape(256, 256), preferred_element_type=F32)
                total = term if total is None else total + term
            dec_o[i] = total.astype(BF)

        @pl.when(i > t)
        def _():
            dec_o[i] = jnp.zeros((576, 256), BF)

    own = g.at[z, py, c]
    copy(own, own, S["cz_s"].at[0], S["cz"].at[0], dev_zp).start()
    copy(own, own, S["cz_s"].at[1], S["cz"].at[1], dev_zm).start()
    to_y(0)
    for n, k in enumerate(slots):
        arrived(rw.at[k, other_half], S["rc"].at[n])

    @pl.loop(0, 4)
    def _(j):
        rwt[j] = rw[:, pl.ds(pl.multiple_of(64 * block_z(j), 64), 64)].reshape(256, WIN).T

    eacc[...] = jnp.zeros_like(eacc)
    y_forward(0)
    arrived(g.at[zm, py, c], S["cz"].at[0])
    part = g.at[zm, py, c, up]
    copy(part, part, S["cz_s"].at[2], S["cz"].at[2], dev_zp).start()
    to_y(1)
    arrived(g.at[zp, py, c], S["cz"].at[1])
    part = g.at[zp, py, c, down]
    copy(part, part, S["cz_s"].at[3], S["cz"].at[3], dev_zm).start()
    to_y(2)
    y_last(0)
    back(0)

    @pl.loop(0, 17)
    def _(k):
        @pl.when(k == 0)
        def _():
            y_forward(1)
            y_forward(2)
            arrived(g.at[z2, py, c, up], S["cz"].at[2])
            arrived(g.at[z2, py, c, down], S["cz"].at[3])
            to_y(3)
            y_last(1)
            back(1)

        @pl.when(k == 1)
        def _():
            y_last(2)
            back(2)

        @pl.when(k == 2)
        def _():
            y_forward(3)

        @pl.when(k == 3)
        def _():
            y_last(3)
            back(3)

        def stage(lag, step, *more):
            @pl.when((k >= lag) & (k < lag + 8))
            def _():
                step(k - lag, *more)

        stage(1, x_second)
        stage(3, x_sum)

        @pl.when((k >= 4) & (k < 8))
        def _():
            q = k - 4
            gt[q] = g[q].reshape(256, 576).T

        stage(4, chain, 1)
        stage(5, chain, 2)
        stage(6, final)
        stage(7, gather, 1)
        stage(8, gather, 2)
        stage(9, gather, 3)

        @pl.when((k >= 8) & (k < 12))
        def _():
            dec_grad(k - 8)

        @pl.when((k >= 10) & (lax.rem(k, 2) == 0))
        def _():
            j = (k - 10) // 2
            eacc[...] += jnp.dot(rwt[j], cg[j].reshape(256, 256), preferred_element_type=F32)

    shift = pl.multiple_of(64 * lax.rem(d, 2), 64)
    enc_o[0] = eacc[pl.ds(shift, 576)].astype(BF)

    @pl.loop(0, 16)
    def _(n):
        p = lax.rem(n, 4)
        b = order(p)
        blk = ss.at[n]

        @pl.when((b <= d) & (d < 3))
        def _():
            sent(blk, S["a_right"].at[n])
            sent(blk, S["e_right"].at[n])

        @pl.when((b >= d) & (d > 0))
        def _():
            sent(blk, S["a_left"].at[n])
            sent(blk, S["e_left"].at[n])

        @pl.when(t < 3)
        def _():
            sent(blk, S["a_n1"].at[n])

        @pl.when(second(b))
        def _():
            sent(blk, S["a_n2"].at[n])

        @pl.when(relays(b))
        def _():
            sent(blk, S["a_rl"].at[n])

        @pl.when(d != b)
        def _():
            sent(blk, S["zc_s"].at[n])

        sent(own, S["cc_s"].at[n])

    @pl.loop(0, 8)
    def _(u):
        @pl.when((t > 0) | (lax.rem(u, 2) == 0))
        def _():
            sent(xr.at[u], S["x_s"].at[u])

        @pl.when(t >= 2)
        def _():
            sent(xr.at[u], S["x_s"].at[8 + u])

        @pl.when(t == 3)
        def _():
            sent(xr.at[u], S["x_s"].at[16 + u])

    @pl.loop(0, 4)
    def _(j):
        sent(po.at[j], S["pc_s"].at[j])
        sent(own, S["cy_s"].at[j * 4])
        sent(own, S["cy_s"].at[j * 4 + 1])
        sent(zst.at[0], S["cy_s"].at[j * 4 + 2])
        sent(zst.at[0], S["cy_s"].at[j * 4 + 3])

    @pl.loop(0, 24)
    def _(n):
        sent(yst.at[n], S["yb_s"].at[n])

    @pl.loop(0, 6)
    def _(n):
        sent(zst.at[n], S["zb_s"].at[n])

    sent(own, S["cz_s"].at[0])
    sent(own, S["cz_s"].at[1])
    sent(zst.at[0], S["cz_s"].at[2])
    sent(zst.at[0], S["cz_s"].at[3])
    for one in col_moves:
        one.wait_send()
    for one in core_moves:
        one.wait_send()


def shards(residual, enc_weight, enc_bias, dec_weight, dec_bias, target):
    wt = jnp.swapaxes(dec_weight[:, 0], 1, 2)
    vmem = pl.BlockSpec(memory_space=pltpu.VMEM)
    hbm = pl.BlockSpec(memory_space=pl.ANY)
    enc, dec = pl.pallas_call(
        body,
        out_shape=(
            jax.ShapeDtypeStruct((1, 576, 256), BF),
            jax.ShapeDtypeStruct((4, 576, 256), BF),
        ),
        in_specs=[hbm, hbm, vmem, hbm, vmem, vmem],
        out_specs=(vmem, vmem),
        scratch_shapes=[pltpu.VMEM(*spec) for spec in SCRATCH.values()]
        + [pltpu.SemaphoreType.DMA((n,)) for n in SEMS.values()],
        compiler_params=pltpu.CompilerParams(
            collective_id=0, has_side_effects=True, vmem_limit_bytes=56 * 1024 * 1024
        ),
    )(residual, enc_weight, enc_bias, wt, dec_bias, target)
    return enc, jnp.swapaxes(dec, 1, 2)[:, None]


def solution(mesh):
    in_specs = (
        P("layer", "dp", None),
        P("layer", None, "feat"),
        P("layer", "feat"),
        P(None, "layer", "feat", "dp"),
        P("layer", "dp"),
        P("layer", "feat", "dp"),
    )
    out_specs = (P("layer", "dp", "feat"), P(None, "layer", "feat", "dp"))
    return jax.shard_map(shards, mesh=mesh, in_specs=in_specs, out_specs=out_specs, check_vma=False)
```

```python
import math

import jax
import jax.numpy as jnp
from jax import lax
from jax.experimental import pallas as pl
from jax.experimental.pallas import tpu as pltpu
from jax.sharding import PartitionSpec as P

MESH = pl.DeviceIdType.MESH
BF = jnp.bfloat16
F32 = jnp.float32
WIN = 640

SEMS = dict(
    load=3, ar=64, az=12, a_n1=16, a_n2=16, a_rl=16,
    rr=4, rr_s=4, rc=3, rc_s=3,
    pc=4, pc_s=4,
    yb=12, yb_s=12, zb=3, zb_s=3,
    cz=3, cz_s=3, cy=12, cy_s=12, cc=4, cc_s=4,
    xr=8, xl=8, xe=8, x_s=24, zc=64, zc_s=16, e=16, e_s=12,
)

SCRATCH = dict(
    resid=((256, 2304), BF), w=((2304, 256), BF), wt=((4, 576, 256), BF),
    pos=((4, 64, 256), F32), codes=((4, 4, 4, 64, 256), BF),
    rw=((4, 256, WIN), BF), rwt=((4, WIN, 256), BF),
    acc=((4, 4, 2, 32, 576), F32), po=((4, 4, 32, 576), BF), pc=((4, 4, 32, 576), BF),
    yst=((12, 32, 576), BF), yb=((12, 32, 576), BF),
    tz=((32, 576), F32), zst=((3, 32, 576), BF), zb=((3, 32, 576), BF),
    g=((4, 4, 2, 32, 576), BF), gt=((4, 576, 256), BF),
    bt=((4, 4, 4, 64, 256), BF), xr=((8, 2, 64, 256), BF), xl=((8, 2, 64, 256), BF), xe=((8, 2, 64, 256), BF),
    s=((8, 2, 64, 256), F32), ss=((16, 64, 256), BF), zc=((4, 16, 64, 256), BF),
    cg=((4, 4, 64, 256), BF), eacc=((WIN, 256), F32),
)


def order(p):
    return jnp.where(p == 0, 0, jnp.where(p == 1, 3, p - 1))


def place(b):
    return jnp.where(b == 0, 0, jnp.where(b == 3, 1, b + 1))


def body(*refs):
    resid_h, w_h, bias, wt_h, dbias, target, enc_o, dec_o = refs[:8]
    R = dict(zip(SCRATCH, refs[8 : 8 + len(SCRATCH)]))
    S = dict(zip(SEMS, refs[8 + len(SCRATCH) :]))
    resid, w, wt, pos, codes = R["resid"], R["w"], R["wt"], R["pos"], R["codes"]
    f = lax.axis_index("feat")
    t = lax.axis_index("layer")
    d = lax.axis_index("dp")
    c, z, y = lax.rem(f, 2), lax.rem(f // 2, 4), f // 8

    def at(yy, zz, core):
        return (lax.rem(yy + 8, 4) * 4 + lax.rem(zz + 8, 4)) * 2 + core

    def along_z(k):
        g = lax.rem(z * 4 + d + k + 16, 16)
        return (at(y, g // 4, c), t, lax.rem(g, 4))

    dev_core = (at(y, z, 1 - c), t, d)
    dev_yp, dev_ym = (at(y + 1, z, c), t, d), (at(y - 1, z, c), t, d)
    dev_zp, dev_zm = (at(y, z + 1, c), t, d), (at(y, z - 1, c), t, d)
    dev_xp, dev_xm = (f, lax.rem(t + 1, 4), d), (f, lax.rem(t + 3, 4), d)
    dev_z2, dev_y2 = (at(y, z + 2, c), t, d), (at(y + 2, z, c), t, d)
    others = [(f, t, lax.rem(d + k, 4)) for k in (1, 2, 3)]
    ym, yp, y2 = lax.rem(y + 3, 4), lax.rem(y + 1, 4), lax.rem(y + 2, 4)
    zm, zp, z2 = lax.rem(z + 3, 4), lax.rem(z + 1, 4), lax.rem(z + 2, 4)
    pd = place(d)

    def copy(src, dst, ssem, rsem, dev):
        return pltpu.make_async_remote_copy(
            src_ref=src, dst_ref=dst, send_sem=ssem, recv_sem=rsem, device_id=dev, device_id_type=MESH
        )

    def arrived(dst, rsem):
        copy(dst, dst, S["load"].at[0], rsem, dev_core).wait_recv()

    def sent(src, ssem):
        copy(src, src, ssem, S["load"].at[0], dev_core).wait_send()

    loads = [
        pltpu.make_async_copy(resid_h.at[0], resid, S["load"].at[0]),
        pltpu.make_async_copy(w_h.at[0], w, S["load"].at[1]),
        pltpu.make_async_copy(wt_h, wt, S["load"].at[2]),
    ]
    for one in loads:
        one.start()

    barrier = pltpu.get_barrier_semaphore()
    partners = [dev_core, dev_yp, dev_ym, dev_zp, dev_zm, dev_xp, dev_xm]
    partners += [dev_y2, dev_z2] + others + [along_z(k) for k in (1, -1, 2, -2)]
    for dev in partners:
        pl.semaphore_signal(barrier, inc=1, device_id=dev, device_id_type=MESH)
    pl.semaphore_wait(barrier, len(partners))

    loads[0].wait()
    loads[1].wait()
    pre = jnp.dot(resid[...], w[...], preferred_element_type=F32) + bias[...]
    positive = jnp.maximum(pre, 0.0)
    pos[...] = positive.reshape(4, 64, 256)
    codes[t, :, pd] = (positive * positive).astype(BF).reshape(4, 64, 256)
    loads[2].wait()

    def chunk_z(i):
        return lax.rem(z + jnp.where(i == 0, 2, jnp.where(i == 1, 1, jnp.where(i == 2, 3, 0))), 4)

    def relays(b):
        side = (b == 0) | (b == 3)
        return ((t == 0) & side) | ((t == 2) & jnp.logical_not(side)) | (t == 3)

    relay_from = jnp.where(t == 3, 0, 1)
    dev_relay = (f, jnp.where(t == 3, 2, 3), d)

    def second(b):
        return (t == 0) | ((t == 1) & ((b == 0) | (b == 3)))

    def to_line(i):
        blk = codes.at[t, chunk_z(i), pd]
        for k, dev in enumerate(others):
            copy(blk, blk, S["az"].at[i * 3 + k], S["ar"].at[t * 16 + i * 4 + pd], dev).start()

    def to_layers(i, b):
        p = place(b)
        n = i * 4 + p
        blk = codes.at[t, chunk_z(i), p]
        sem = S["ar"].at[t * 16 + n]

        @pl.when(t < 3)
        def _():
            copy(blk, blk, S["a_n1"].at[n], sem, dev_xp).start()

        @pl.when(second(b))
        def _():
            copy(blk, blk, S["a_n2"].at[n], sem, dev_xm).start()

    def relay(i, b):
        @pl.when(relays(b))
        def _():
            p = place(b)
            blk = codes.at[relay_from, chunk_z(i), p]
            sem = S["ar"].at[relay_from * 16 + i * 4 + p]
            arrived(blk, sem)
            copy(blk, blk, S["a_rl"].at[i * 4 + p], sem, dev_relay).start()

    rw, rwt = R["rw"], R["rwt"]

    def start_col(k):
        return pl.multiple_of(k * 576 - 64 * lax.rem(k, 2), 128)

    def move_cols(k, lo, size, slot):
        rows = pl.ds(pl.multiple_of(c * 128 + lo, 64), size)
        dev = along_z(k)
        src = resid.at[rows, pl.ds(start_col(dev[2]), WIN)]
        return copy(src, rw.at[pd, rows], S["rr_s"].at[slot], S["rr"].at[slot], dev)

    col_moves = [move_cols(1, 0, 128, 0), move_cols(-1, 0, 128, 1), move_cols(2, 0, 64, 2), move_cols(-2, 64, 64, 3)]
    half = pl.ds(pl.multiple_of(c * 128, 128), 128)
    other_half = pl.ds(pl.multiple_of((1 - c) * 128, 128), 128)
    slots = [place(lax.rem(d + k, 4)) for k in (3, 1, 2)]
    core_moves = [
        copy(rw.at[k, half], rw.at[k, half], S["rc_s"].at[n], S["rc"].at[n], dev_core) for n, k in enumerate(slots)
    ]

    acc, po, pc = R["acc"], R["po"], R["pc"]

    def recon_chunk(i):
        zz = chunk_z(i)

        @pl.loop(0, 12)
        def _(n):
            l, p = n // 4, lax.rem(n, 4)
            relayed = relays(order(p)) & (l == relay_from)

            @pl.when((l < t) & jnp.logical_not(relayed))
            def _():
                arrived(codes.at[l, zz, p], S["ar"].at[l * 16 + i * 4 + p])

        for top in range(4):
            @pl.when(t == top)
            def _():
                total = None
                for l in range(top + 1):
                    term = lax.dot_general(
                        codes[l, zz].reshape(256, 256), wt[l], (((1,), (1,)), ((), ())), preferred_element_type=F32
                    )
                    total = term if total is None else total + term
                acc[i] = total.reshape(4, 2, 32, 576)

        po[i] = acc[i, :, 1 - c].astype(BF)
        copy(po.at[i], pc.at[i], S["pc_s"].at[i], S["pc"].at[i], dev_core).start()

    yst, yb = R["yst"], R["yb"]

    def partial(i, yy):
        p = place(yy)
        return acc[i, p, c] + pc[i, p].astype(F32)

    def y_part(i):
        arrived(pc.at[i], S["pc"].at[i])
        for k, (yy, dev) in enumerate(((yp, dev_yp), (ym, dev_ym), (y2, dev_y2))):
            n = i * 3 + k
            yst[n] = partial(i, yy).astype(BF)
            copy(yst.at[n], yb.at[n], S["yb_s"].at[n], S["yb"].at[n], dev).start()

    tz, zst, zb = R["tz"], R["zst"], R["zb"]

    def z_part(i):
        total = partial(i, y)
        for k in range(3):
            n = i * 3 + k
            arrived(yb.at[n], S["yb"].at[n])
            total = total + yb[n].astype(F32)
        tz[...] = total

        for k, dev in enumerate((dev_z2, dev_zp, dev_zm)):
            @pl.when(i == k)
            def _():
                zst[k] = total.astype(BF)
                copy(zst.at[k], zb.at[k], S["zb_s"].at[k], S["zb"].at[k], dev).start()

    for i in range(4):
        to_line(i)
    for i in range(2):
        to_layers(i, d)

    @pl.loop(0, 8)
    def _(k):
        @pl.when((k >= 4) & (k < 8))
        def _():
            z_part(k - 4)

        @pl.when((k >= 3) & (k < 7))
        def _():
            y_part(k - 3)

        @pl.when(k < 4)
        def _():
            for h in range(1, 4):
                for b in (d - h, d + h):
                    @pl.when((b >= 0) & (b < 4))
                    def _():
                        p = place(b)
                        arrived(codes.at[t, chunk_z(k), p], S["ar"].at[t * 16 + k * 4 + p])
                        to_layers(k, b)

        @pl.when(k < 2)
        def _():
            to_layers(k + 2, d)

        @pl.when((k >= 1) & (k < 5))
        def _():
            relay(k - 1, d)
            for h in range(1, 4):
                for b in (d - h, d + h):
                    @pl.when((b >= 0) & (b < 4))
                    def _():
                        relay(k - 1, b)

        @pl.when((k >= 2) & (k < 6))
        def _():
            recon_chunk(k - 2)

        @pl.when(k == 3)
        def _():
            for one in col_moves:
                one.start()
            rw[pd] = resid[:, pl.ds(start_col(d), WIN)]

        @pl.when(k == 6)
        def _():
            arrived(rw.at[slots[0], half], S["rr"].at[0])
            arrived(rw.at[slots[1], half], S["rr"].at[1])
            arrived(rw.at[slots[2], pl.ds(pl.multiple_of(c * 128, 64), 64)], S["rr"].at[2])
            arrived(rw.at[slots[2], pl.ds(pl.multiple_of(c * 128 + 64, 64), 64)], S["rr"].at[3])
            for one in core_moves:
                one.start()

    scale = 1.0 / math.sqrt(1024)
    g = R["g"]
    py = place(y)
    recon = tz[...]
    for k in range(3):
        arrived(zb.at[k], S["zb"].at[k])
        recon = recon + zb[k].astype(F32)
    g[z, py, c] = ((recon + dbias[...] - target[0].astype(F32)) * scale).astype(BF)

    def block_z(j):
        return lax.rem(z + jnp.where(j == 0, 0, jnp.where(j == 1, 3, jnp.where(j == 2, 1, 2))), 4)

    def to_y(j):
        blk = g.at[block_z(j), py, c]
        for k, dev in enumerate((dev_yp, dev_ym, dev_y2)):
            copy(blk, blk, S["cy_s"].at[j * 3 + k], S["cy"].at[j * 3 + k], dev).start()

    def from_z(j):
        arrived(g.at[block_z(j), py, c], S["cz"].at[j - 1])
        to_y(j)

    def from_y(j):
        for k, yy in enumerate((ym, yp, y2)):
            arrived(g.at[block_z(j), place(yy), c], S["cy"].at[j * 3 + k])
        blk = g.at[block_z(j), :, c]
        copy(blk, blk, S["cc_s"].at[j], S["cc"].at[j], dev_core).start()

    bt, xr, xl, xe, s, ss, zc = R["bt"], R["xr"], R["xl"], R["xe"], R["s"], R["ss"], R["zc"]
    gt, cg, eacc = R["gt"], R["cg"], R["eacc"]

    def x_send(k, u, l, dst, name, dev):
        src = bt.at[l, u // 2, pl.ds(2 * lax.rem(u, 2), 2)]
        copy(src, dst.at[u], S["x_s"].at[k * 8 + u], S[name].at[u], dev).start()

    def back(j):
        zz = block_z(j)

        arrived(g.at[zz, :, 1 - c], S["cc"].at[j])

        @pl.loop(0, t + 1)
        def _(l):
            term = jnp.dot(g[zz].reshape(256, 576), wt[l], preferred_element_type=F32)
            bt[l, j] = term.astype(BF).reshape(4, 64, 256)

        for h in range(2):
            u = j * 2 + h

            @pl.when(t == 1)
            def _():
                x_send(0, u, 0, xr, "xr", dev_xm)

            @pl.when(t == 2)
            def _():
                x_send(0, u, 0, xl, "xl", dev_xp)
                if h == 0:
                    x_send(1, u, 1, xr, "xr", dev_xm)

            @pl.when(t == 3)
            def _():
                x_send(1, u, 1, xe, "xe", dev_xp if h == 0 else dev_xm)
                x_send(2, u, 2, xr, "xr", dev_xm)

    def add_in(l, u, other, name):
        arrived(other.at[u], S[name].at[u])
        j, part = u // 2, pl.ds(2 * lax.rem(u, 2), 2)
        bt[l, j, part] = (bt[l, j, part].astype(F32) + other[u].astype(F32)).astype(BF)

    def x_second(u):
        h = lax.rem(u, 2)

        @pl.when(t == 3)
        def _():
            add_in(0, u, xl, "xl")
            x_send(0, u, 0, xl, "xl", dev_xp)

        @pl.when((t == 2) & (h == 1))
        def _():
            add_in(1, u, xe, "xe")
            x_send(1, u, 1, xr, "xr", dev_xm)

        @pl.when((t == 0) & (h == 0))
        def _():
            arrived(xe.at[u], S["xe"].at[u])
            copy(xe.at[u], xl.at[u], S["x_s"].at[u], S["xl"].at[u], dev_xp).start()

    def x_sum(u):
        h = lax.rem(u, 2)
        s[u] = bt[t, u // 2, pl.ds(2 * h, 2)].astype(F32)

        @pl.when(t < 3)
        def _():
            arrived(xr.at[u], S["xr"].at[u])
            s[u] += xr[u].astype(F32)

        @pl.when((t == 0) | ((t == 1) & (h == 0)))
        def _():
            arrived(xl.at[u], S["xl"].at[u])
            s[u] += xl[u].astype(F32)

        @pl.loop(0, 2)
        def _(r):
            p = 2 * h + r
            n = (u // 2) * 4 + p
            q = order(p)

            @pl.when(q != d)
            def _():
                ss[n] = s[u, r].astype(BF)
                copy(ss.at[n], zc.at[d, n], S["zc_s"].at[n], S["zc"].at[d * 16 + n], (f, t, q)).start()

    def final(u):
        @pl.when(pd // 2 == lax.rem(u, 2))
        def _():
            j = u // 2
            n = j * 4 + pd
            total = s[u, lax.rem(pd, 2)]
            for k in (1, 3, 2):
                q = lax.rem(d + k, 4)
                arrived(zc.at[q, n], S["zc"].at[q * 16 + n])
                total = total + zc[q, n].astype(F32)

            cg[j, pd] = (total * 2.0 * pos[block_z(j)]).astype(BF)
            blk = cg.at[j, pd]
            for k, dev in enumerate(others):
                copy(blk, blk, S["e_s"].at[j * 3 + k], S["e"].at[n], dev).start()

    def gather(u):
        @pl.loop(0, 2)
        def _(r):
            p = 2 * lax.rem(u, 2) + r

            @pl.when(p != pd)
            def _():
                arrived(cg.at[u // 2, p], S["e"].at[(u // 2) * 4 + p])

    def dec_grad(i):
        @pl.when(i <= t)
        def _():
            total = None
            for k in range(4):
                term = jnp.dot(gt[k], codes[i, k].reshape(256, 256), preferred_element_type=F32)
                total = term if total is None else total + term
            dec_o[i] = total.astype(BF)

        @pl.when(i > t)
        def _():
            dec_o[i] = jnp.zeros((576, 256), BF)

    own = g.at[z, py, c]
    for k, dev in enumerate((dev_zp, dev_zm, dev_z2)):
        copy(own, own, S["cz_s"].at[k], S["cz"].at[k], dev).start()
    to_y(0)
    for n, k in enumerate(slots):
        arrived(rw.at[k, other_half], S["rc"].at[n])

    @pl.loop(0, 4)
    def _(j):
        rwt[j] = rw[:, pl.ds(pl.multiple_of(64 * block_z(j), 64), 64)].reshape(256, WIN).T

    eacc[...] = jnp.zeros_like(eacc)
    from_y(0)
    from_z(1)
    from_z(2)
    back(0)
    from_z(3)
    from_y(1)
    from_y(2)
    back(1)

    @pl.loop(0, 14)
    def _(k):
        def stage(lag, step):
            @pl.when((k >= lag) & (k < lag + 8))
            def _():
                step(k - lag)

        stage(6, gather)

        @pl.when((k >= 7) & (lax.rem(k, 2) == 1))
        def _():
            j = (k - 7) // 2
            eacc[...] += jnp.dot(rwt[j], cg[j].reshape(256, 256), preferred_element_type=F32)

        stage(4, final)
        stage(2, x_sum)
        stage(0, x_second)

        @pl.when(k == 0)
        def _():
            back(2)

        @pl.when(k == 1)
        def _():
            from_y(3)
            back(3)

        @pl.when((k >= 2) & (k < 4))
        def _():
            for q in (2 * k - 4, 2 * k - 3):
                gt[q] = g[q].reshape(256, 576).T

        @pl.when((k >= 4) & (k < 8))
        def _():
            dec_grad(k - 4)

    shift = pl.multiple_of(64 * lax.rem(d, 2), 64)
    enc_o[0] = eacc[pl.ds(shift, 576)].astype(BF)

    @pl.loop(0, 16)
    def _(n):
        b = order(lax.rem(n, 4))
        blk = ss.at[n]

        @pl.when(t < 3)
        def _():
            sent(blk, S["a_n1"].at[n])

        @pl.when(second(b))
        def _():
            sent(blk, S["a_n2"].at[n])

        @pl.when(relays(b))
        def _():
            sent(blk, S["a_rl"].at[n])

        @pl.when(d != b)
        def _():
            sent(blk, S["zc_s"].at[n])

    @pl.loop(0, 12)
    def _(n):
        sent(ss.at[0], S["az"].at[n])
        sent(ss.at[0], S["e_s"].at[n])
        sent(own, S["yb_s"].at[n])
        sent(own, S["cy_s"].at[n])

    @pl.loop(0, 8)
    def _(u):
        @pl.when((t > 0) | (lax.rem(u, 2) == 0))
        def _():
            sent(xr.at[u], S["x_s"].at[u])

        @pl.when(t >= 2)
        def _():
            sent(xr.at[u], S["x_s"].at[8 + u])

        @pl.when(t == 3)
        def _():
            sent(xr.at[u], S["x_s"].at[16 + u])

    @pl.loop(0, 4)
    def _(j):
        sent(po.at[j], S["pc_s"].at[j])
        sent(po.at[j], S["cc_s"].at[j])

    for k in range(3):
        sent(own, S["zb_s"].at[k])
        sent(own, S["cz_s"].at[k])
        col_moves[k].wait_send()
        core_moves[k].wait_send()
    col_moves[3].wait_send()


def shards(residual, enc_weight, enc_bias, dec_weight, dec_bias, target):
    wt = jnp.swapaxes(dec_weight[:, 0], 1, 2)
    vmem = pl.BlockSpec(memory_space=pltpu.VMEM)
    hbm = pl.BlockSpec(memory_space=pl.ANY)
    enc, dec = pl.pallas_call(
        body,
        out_shape=(
            jax.ShapeDtypeStruct((1, 576, 256), BF),
            jax.ShapeDtypeStruct((4, 576, 256), BF),
        ),
        in_specs=[hbm, hbm, vmem, hbm, vmem, vmem],
        out_specs=(vmem, vmem),
        scratch_shapes=[pltpu.VMEM(*spec) for spec in SCRATCH.values()]
        + [pltpu.SemaphoreType.DMA((n,)) for n in SEMS.values()],
        compiler_params=pltpu.CompilerParams(
            collective_id=0, has_side_effects=True, vmem_limit_bytes=56 * 1024 * 1024
        ),
    )(residual, enc_weight, enc_bias, wt, dec_bias, target)
    return enc, jnp.swapaxes(dec, 1, 2)[:, None]


def solution(mesh):
    in_specs = (
        P("layer", "dp", None),
        P("layer", None, "feat"),
        P("layer", "feat"),
        P(None, "layer", "feat", "dp"),
        P("layer", "dp"),
        P("layer", "feat", "dp"),
    )
    out_specs = (P("layer", "dp", "feat"), P(None, "layer", "feat", "dp"))
    return jax.shard_map(shards, mesh=mesh, in_specs=in_specs, out_specs=out_specs, check_vma=False)
```

```python
import math

import jax
import jax.numpy as jnp
from jax import lax
from jax.experimental import pallas as pl
from jax.experimental.pallas import tpu as pltpu
from jax.sharding import PartitionSpec as P

MESH = pl.DeviceIdType.MESH
BF = jnp.bfloat16
F32 = jnp.float32
WIN = 640

SEMS = dict(
    load=3, ar=64, az=12, a_n1=16, a_n2=16, a_rl=16,
    rr=4, rr_s=4, rc=3, rc_s=3,
    pc=4, pc_s=4,
    yb=12, yb_s=12, zb=3, zb_s=3,
    cz=3, cz_s=3, cy=12, cy_s=12, cc=4, cc_s=4,
    xr=8, xl=8, xe=8, x_s=24, zc=64, zc_s=16, e=16, e_s=12,
)

SCRATCH = dict(
    resid=((256, 2304), BF), w=((2304, 256), BF), wt=((4, 576, 256), BF),
    pos=((4, 64, 256), F32), codes=((4, 4, 4, 64, 256), BF),
    rw=((4, 256, WIN), BF), rwt=((4, WIN, 256), BF),
    acc=((4, 4, 2, 32, 576), F32), po=((4, 4, 32, 576), BF), pc=((4, 4, 32, 576), BF),
    yst=((12, 32, 576), BF), yb=((12, 32, 576), BF),
    tz=((32, 576), F32), zst=((3, 32, 576), BF), zb=((3, 32, 576), BF),
    g=((4, 4, 2, 32, 576), BF), gt=((4, 576, 256), BF),
    bt=((4, 4, 4, 64, 256), BF), xr=((8, 2, 64, 256), BF), xl=((8, 2, 64, 256), BF), xe=((8, 2, 64, 256), BF),
    s=((8, 2, 64, 256), F32), ss=((16, 64, 256), BF), zc=((4, 16, 64, 256), BF),
    cg=((4, 4, 64, 256), BF), eacc=((WIN, 256), F32),
)


def order(p):
    return jnp.where(p == 0, 0, jnp.where(p == 1, 3, p - 1))


def place(b):
    return jnp.where(b == 0, 0, jnp.where(b == 3, 1, b + 1))


def body(*refs):
    resid_h, w_h, bias, wt_h, dbias, target, enc_o, dec_o = refs[:8]
    R = dict(zip(SCRATCH, refs[8 : 8 + len(SCRATCH)]))
    S = dict(zip(SEMS, refs[8 + len(SCRATCH) :]))
    resid, w, wt, pos, codes = R["resid"], R["w"], R["wt"], R["pos"], R["codes"]
    f = lax.axis_index("feat")
    t = lax.axis_index("layer")
    d = lax.axis_index("dp")
    c, z, y = lax.rem(f, 2), lax.rem(f // 2, 4), f // 8

    def at(yy, zz, core):
        return (lax.rem(yy + 8, 4) * 4 + lax.rem(zz + 8, 4)) * 2 + core

    def along_z(k):
        g = lax.rem(z * 4 + d + k + 16, 16)
        return (at(y, g // 4, c), t, lax.rem(g, 4))

    dev_core = (at(y, z, 1 - c), t, d)
    dev_yp, dev_ym = (at(y + 1, z, c), t, d), (at(y - 1, z, c), t, d)
    dev_zp, dev_zm = (at(y, z + 1, c), t, d), (at(y, z - 1, c), t, d)
    dev_xp, dev_xm = (f, lax.rem(t + 1, 4), d), (f, lax.rem(t + 3, 4), d)
    dev_z2, dev_y2 = (at(y, z + 2, c), t, d), (at(y + 2, z, c), t, d)
    others = [(f, t, lax.rem(d + k, 4)) for k in (1, 2, 3)]
    ym, yp, y2 = lax.rem(y + 3, 4), lax.rem(y + 1, 4), lax.rem(y + 2, 4)
    zm, zp, z2 = lax.rem(z + 3, 4), lax.rem(z + 1, 4), lax.rem(z + 2, 4)
    pd = place(d)

    def copy(src, dst, ssem, rsem, dev):
        return pltpu.make_async_remote_copy(
            src_ref=src, dst_ref=dst, send_sem=ssem, recv_sem=rsem, device_id=dev, device_id_type=MESH
        )

    def arrived(dst, rsem):
        copy(dst, dst, S["load"].at[0], rsem, dev_core).wait_recv()

    def sent(src, ssem):
        copy(src, src, ssem, S["load"].at[0], dev_core).wait_send()

    loads = [
        pltpu.make_async_copy(resid_h.at[0], resid, S["load"].at[0]),
        pltpu.make_async_copy(w_h.at[0], w, S["load"].at[1]),
        pltpu.make_async_copy(wt_h, wt, S["load"].at[2]),
    ]
    for one in loads:
        one.start()

    barrier = pltpu.get_barrier_semaphore()
    partners = [dev_core, dev_yp, dev_ym, dev_zp, dev_zm, dev_xp, dev_xm]
    partners += [dev_y2, dev_z2] + others + [along_z(k) for k in (1, -1, 2, -2)]
    for dev in partners:
        pl.semaphore_signal(barrier, inc=1, device_id=dev, device_id_type=MESH)
    pl.semaphore_wait(barrier, len(partners))

    loads[0].wait()
    loads[1].wait()
    pre = jnp.dot(resid[...], w[...], preferred_element_type=F32) + bias[...]
    positive = jnp.maximum(pre, 0.0)
    pos[...] = positive.reshape(4, 64, 256)
    codes[t, :, pd] = (positive * positive).astype(BF).reshape(4, 64, 256)
    loads[2].wait()

    def chunk_z(i):
        return lax.rem(z + jnp.where(i == 0, 2, jnp.where(i == 1, 1, jnp.where(i == 2, 3, 0))), 4)

    def relays(b):
        side = (b == 0) | (b == 3)
        return ((t == 0) & side) | ((t == 2) & jnp.logical_not(side)) | (t == 3)

    relay_from = jnp.where(t == 3, 0, 1)
    dev_relay = (f, jnp.where(t == 3, 2, 3), d)

    def second(b):
        return (t == 0) | ((t == 1) & ((b == 0) | (b == 3)))

    def to_line(i):
        blk = codes.at[t, chunk_z(i), pd]
        for k, dev in enumerate(others):
            copy(blk, blk, S["az"].at[i * 3 + k], S["ar"].at[t * 16 + i * 4 + pd], dev).start()

    def to_layers(i, b):
        p = place(b)
        n = i * 4 + p
        blk = codes.at[t, chunk_z(i), p]
        sem = S["ar"].at[t * 16 + n]

        @pl.when(t < 3)
        def _():
            copy(blk, blk, S["a_n1"].at[n], sem, dev_xp).start()

        @pl.when(second(b))
        def _():
            copy(blk, blk, S["a_n2"].at[n], sem, dev_xm).start()

    def relay(i, b):
        @pl.when(relays(b))
        def _():
            p = place(b)
            blk = codes.at[relay_from, chunk_z(i), p]
            sem = S["ar"].at[relay_from * 16 + i * 4 + p]
            arrived(blk, sem)
            copy(blk, blk, S["a_rl"].at[i * 4 + p], sem, dev_relay).start()

    rw, rwt = R["rw"], R["rwt"]

    def start_col(k):
        return pl.multiple_of(k * 576 - 64 * lax.rem(k, 2), 128)

    def move_cols(k, lo, size, slot):
        rows = pl.ds(pl.multiple_of(c * 128 + lo, 64), size)
        dev = along_z(k)
        src = resid.at[rows, pl.ds(start_col(dev[2]), WIN)]
        return copy(src, rw.at[pd, rows], S["rr_s"].at[slot], S["rr"].at[slot], dev)

    col_moves = [move_cols(1, 0, 128, 0), move_cols(-1, 0, 128, 1), move_cols(2, 0, 64, 2), move_cols(-2, 64, 64, 3)]
    half = pl.ds(pl.multiple_of(c * 128, 128), 128)
    other_half = pl.ds(pl.multiple_of((1 - c) * 128, 128), 128)
    slots = [place(lax.rem(d + k, 4)) for k in (3, 1, 2)]
    core_moves = [
        copy(rw.at[k, half], rw.at[k, half], S["rc_s"].at[n], S["rc"].at[n], dev_core) for n, k in enumerate(slots)
    ]

    acc, po, pc = R["acc"], R["po"], R["pc"]

    def recon_chunk(i):
        zz = chunk_z(i)

        @pl.loop(0, 12)
        def _(n):
            l, p = n // 4, lax.rem(n, 4)
            relayed = relays(order(p)) & (l == relay_from)

            @pl.when((l < t) & jnp.logical_not(relayed))
            def _():
                arrived(codes.at[l, zz, p], S["ar"].at[l * 16 + i * 4 + p])

        for top in range(4):
            @pl.when(t == top)
            def _():
                total = None
                for l in range(top + 1):
                    term = lax.dot_general(
                        codes[l, zz].reshape(256, 256), wt[l], (((1,), (1,)), ((), ())), preferred_element_type=F32
                    )
                    total = term if total is None else total + term
                acc[i] = total.reshape(4, 2, 32, 576)

        po[i] = acc[i, :, 1 - c].astype(BF)
        copy(po.at[i], pc.at[i], S["pc_s"].at[i], S["pc"].at[i], dev_core).start()

    yst, yb = R["yst"], R["yb"]

    def partial(i, yy):
        p = place(yy)
        return acc[i, p, c] + pc[i, p].astype(F32)

    def y_part(i):
        arrived(pc.at[i], S["pc"].at[i])
        for k, (yy, dev) in enumerate(((yp, dev_yp), (ym, dev_ym), (y2, dev_y2))):
            n = i * 3 + k
            yst[n] = partial(i, yy).astype(BF)
            copy(yst.at[n], yb.at[n], S["yb_s"].at[n], S["yb"].at[n], dev).start()

    tz, zst, zb = R["tz"], R["zst"], R["zb"]

    def z_part(i):
        total = partial(i, y)
        for k in range(3):
            n = i * 3 + k
            arrived(yb.at[n], S["yb"].at[n])
            total = total + yb[n].astype(F32)
        tz[...] = total

        for k, dev in enumerate((dev_z2, dev_zp, dev_zm)):
            @pl.when(i == k)
            def _():
                zst[k] = total.astype(BF)
                copy(zst.at[k], zb.at[k], S["zb_s"].at[k], S["zb"].at[k], dev).start()

    for i in range(4):
        to_line(i)
    for i in range(4):
        to_layers(i, d)

    @pl.loop(0, 8)
    def _(k):
        @pl.when(k < 4)
        def _():
            for h in range(1, 4):
                for b in (d - h, d + h):
                    @pl.when((b >= 0) & (b < 4))
                    def _():
                        p = place(b)
                        arrived(codes.at[t, chunk_z(k), p], S["ar"].at[t * 16 + k * 4 + p])
                        to_layers(k, b)

        @pl.when((k >= 1) & (k < 5))
        def _():
            relay(k - 1, d)
            for h in range(1, 4):
                for b in (d - h, d + h):
                    @pl.when((b >= 0) & (b < 4))
                    def _():
                        relay(k - 1, b)

        @pl.when((k >= 4) & (k < 8))
        def _():
            z_part(k - 4)

        @pl.when((k >= 3) & (k < 7))
        def _():
            y_part(k - 3)

        @pl.when((k >= 2) & (k < 6))
        def _():
            recon_chunk(k - 2)

    scale = 1.0 / math.sqrt(1024)
    g = R["g"]
    py = place(y)
    recon = tz[...]
    for k in range(3):
        arrived(zb.at[k], S["zb"].at[k])
        recon = recon + zb[k].astype(F32)
    g[z, py, c] = ((recon + dbias[...] - target[0].astype(F32)) * scale).astype(BF)

    def block_z(j):
        return lax.rem(z + jnp.where(j == 0, 0, jnp.where(j == 1, 3, jnp.where(j == 2, 1, 2))), 4)

    def to_y(j):
        blk = g.at[block_z(j), py, c]
        for k, dev in enumerate((dev_yp, dev_ym, dev_y2)):
            copy(blk, blk, S["cy_s"].at[j * 3 + k], S["cy"].at[j * 3 + k], dev).start()

    def from_z(j):
        arrived(g.at[block_z(j), py, c], S["cz"].at[j - 1])
        to_y(j)

    def from_y(j):
        for k, yy in enumerate((ym, yp, y2)):
            arrived(g.at[block_z(j), place(yy), c], S["cy"].at[j * 3 + k])
        blk = g.at[block_z(j), :, c]
        copy(blk, blk, S["cc_s"].at[j], S["cc"].at[j], dev_core).start()

    bt, xr, xl, xe, s, ss, zc = R["bt"], R["xr"], R["xl"], R["xe"], R["s"], R["ss"], R["zc"]
    gt, cg, eacc = R["gt"], R["cg"], R["eacc"]

    def x_send(k, u, l, dst, name, dev):
        src = bt.at[l, u // 2, pl.ds(2 * lax.rem(u, 2), 2)]
        copy(src, dst.at[u], S["x_s"].at[k * 8 + u], S[name].at[u], dev).start()

    def back(j):
        zz = block_z(j)

        arrived(g.at[zz, :, 1 - c], S["cc"].at[j])

        @pl.loop(0, t + 1)
        def _(l):
            term = jnp.dot(g[zz].reshape(256, 576), wt[l], preferred_element_type=F32)
            bt[l, j] = term.astype(BF).reshape(4, 64, 256)

        for h in range(2):
            u = j * 2 + h

            @pl.when(t == 1)
            def _():
                x_send(0, u, 0, xr, "xr", dev_xm)

            @pl.when(t == 2)
            def _():
                x_send(0, u, 0, xl, "xl", dev_xp)
                if h == 0:
                    x_send(1, u, 1, xr, "xr", dev_xm)

            @pl.when(t == 3)
            def _():
                x_send(1, u, 1, xe, "xe", dev_xp if h == 0 else dev_xm)
                x_send(2, u, 2, xr, "xr", dev_xm)

    def add_in(l, u, other, name):
        arrived(other.at[u], S[name].at[u])
        j, part = u // 2, pl.ds(2 * lax.rem(u, 2), 2)
        bt[l, j, part] = (bt[l, j, part].astype(F32) + other[u].astype(F32)).astype(BF)

    def x_second(u):
        h = lax.rem(u, 2)

        @pl.when(t == 3)
        def _():
            add_in(0, u, xl, "xl")
            x_send(0, u, 0, xl, "xl", dev_xp)

        @pl.when((t == 2) & (h == 1))
        def _():
            add_in(1, u, xe, "xe")
            x_send(1, u, 1, xr, "xr", dev_xm)

        @pl.when((t == 0) & (h == 0))
        def _():
            arrived(xe.at[u], S["xe"].at[u])
            copy(xe.at[u], xl.at[u], S["x_s"].at[u], S["xl"].at[u], dev_xp).start()

    def x_sum(u):
        h = lax.rem(u, 2)
        s[u] = bt[t, u // 2, pl.ds(2 * h, 2)].astype(F32)

        @pl.when(t < 3)
        def _():
            arrived(xr.at[u], S["xr"].at[u])
            s[u] += xr[u].astype(F32)

        @pl.when((t == 0) | ((t == 1) & (h == 0)))
        def _():
            arrived(xl.at[u], S["xl"].at[u])
            s[u] += xl[u].astype(F32)

        @pl.loop(0, 2)
        def _(r):
            p = 2 * h + r
            n = (u // 2) * 4 + p
            q = order(p)

            @pl.when(q != d)
            def _():
                ss[n] = s[u, r].astype(BF)
                copy(ss.at[n], zc.at[d, n], S["zc_s"].at[n], S["zc"].at[d * 16 + n], (f, t, q)).start()

    def final(u):
        @pl.when(pd // 2 == lax.rem(u, 2))
        def _():
            j = u // 2
            n = j * 4 + pd
            total = s[u, lax.rem(pd, 2)]
            for k in (1, 3, 2):
                q = lax.rem(d + k, 4)
                arrived(zc.at[q, n], S["zc"].at[q * 16 + n])
                total = total + zc[q, n].astype(F32)

            cg[j, pd] = (total * 2.0 * pos[block_z(j)]).astype(BF)
            blk = cg.at[j, pd]
            for k, dev in enumerate(others):
                copy(blk, blk, S["e_s"].at[j * 3 + k], S["e"].at[n], dev).start()

    def gather(u):
        @pl.loop(0, 2)
        def _(r):
            p = 2 * lax.rem(u, 2) + r

            @pl.when(p != pd)
            def _():
                arrived(cg.at[u // 2, p], S["e"].at[(u // 2) * 4 + p])

    def dec_grad(i):
        @pl.when(i <= t)
        def _():
            total = None
            for k in range(4):
                term = jnp.dot(gt[k], codes[i, k].reshape(256, 256), preferred_element_type=F32)
                total = term if total is None else total + term
            dec_o[i] = total.astype(BF)

        @pl.when(i > t)
        def _():
            dec_o[i] = jnp.zeros((576, 256), BF)

    own = g.at[z, py, c]
    for k, dev in enumerate((dev_zp, dev_zm, dev_z2)):
        copy(own, own, S["cz_s"].at[k], S["cz"].at[k], dev).start()
    to_y(0)
    eacc[...] = jnp.zeros_like(eacc)
    from_y(0)
    from_z(1)
    from_z(2)
    back(0)
    from_y(1)
    back(1)
    from_y(2)

    @pl.loop(0, 7)
    def _(k):
        def stage(lag, step):
            @pl.when((k >= lag) & (k < lag + 4))
            def _():
                j = k - lag
                step(2 * j)
                step(2 * j + 1)

        stage(0, x_second)

        @pl.when(k == 0)
        def _():
            back(2)
            from_z(3)
            for one in col_moves:
                one.start()
            rw[pd] = resid[:, pl.ds(start_col(d), WIN)]

        @pl.when(k == 1)
        def _():
            from_y(3)
            back(3)

        @pl.when(k == 2)
        def _():
            for q in range(4):
                gt[q] = g[q].reshape(256, 576).T

        @pl.when((k >= 3) & (k < 5))
        def _():
            dec_grad(2 * k - 6)
            dec_grad(2 * k - 5)

        stage(1, x_sum)

        @pl.when(k == 2)
        def _():
            arrived(rw.at[slots[0], half], S["rr"].at[0])
            arrived(rw.at[slots[1], half], S["rr"].at[1])
            arrived(rw.at[slots[2], pl.ds(pl.multiple_of(c * 128, 64), 64)], S["rr"].at[2])
            arrived(rw.at[slots[2], pl.ds(pl.multiple_of(c * 128 + 64, 64), 64)], S["rr"].at[3])
            for one in core_moves:
                one.start()

        stage(2, final)

        @pl.when(k == 3)
        def _():
            for n, m in enumerate(slots):
                arrived(rw.at[m, other_half], S["rc"].at[n])

            @pl.loop(0, 4)
            def _(j):
                rwt[j] = rw[:, pl.ds(pl.multiple_of(64 * block_z(j), 64), 64)].reshape(256, WIN).T

        stage(3, gather)

        @pl.when(k >= 3)
        def _():
            eacc[...] += jnp.dot(rwt[k - 3], cg[k - 3].reshape(256, 256), preferred_element_type=F32)

    shift = pl.multiple_of(64 * lax.rem(d, 2), 64)
    enc_o[0] = eacc[pl.ds(shift, 576)].astype(BF)

    @pl.loop(0, 16)
    def _(n):
        b = order(lax.rem(n, 4))
        blk = ss.at[n]

        @pl.when(t < 3)
        def _():
            sent(blk, S["a_n1"].at[n])

        @pl.when(second(b))
        def _():
            sent(blk, S["a_n2"].at[n])

        @pl.when(relays(b))
        def _():
            sent(blk, S["a_rl"].at[n])

        @pl.when(d != b)
        def _():
            sent(blk, S["zc_s"].at[n])

    @pl.loop(0, 12)
    def _(n):
        sent(ss.at[0], S["az"].at[n])
        sent(ss.at[0], S["e_s"].at[n])
        sent(own, S["yb_s"].at[n])
        sent(own, S["cy_s"].at[n])

    @pl.loop(0, 8)
    def _(u):
        @pl.when((t > 0) | (lax.rem(u, 2) == 0))
        def _():
            sent(xr.at[u], S["x_s"].at[u])

        @pl.when(t >= 2)
        def _():
            sent(xr.at[u], S["x_s"].at[8 + u])

        @pl.when(t == 3)
        def _():
            sent(xr.at[u], S["x_s"].at[16 + u])

    @pl.loop(0, 4)
    def _(j):
        sent(po.at[j], S["pc_s"].at[j])
        sent(po.at[j], S["cc_s"].at[j])

    for k in range(3):
        sent(own, S["zb_s"].at[k])
        sent(own, S["cz_s"].at[k])
        col_moves[k].wait_send()
        core_moves[k].wait_send()
    col_moves[3].wait_send()


def copy_out(enc, dec, enc_o, dec_o, sems):
    moves = [pltpu.make_async_copy(enc, enc_o, sems.at[0]), pltpu.make_async_copy(dec, dec_o, sems.at[1])]
    for one in moves:
        one.start()
    for one in moves:
        one.wait()


def shards(residual, enc_weight, enc_bias, dec_weight, dec_bias, target):
    wt = jnp.swapaxes(dec_weight[:, 0], 1, 2)
    vmem = pl.BlockSpec(memory_space=pltpu.VMEM)
    hbm = pl.BlockSpec(memory_space=pl.ANY)
    enc, dec = pl.pallas_call(
        body,
        out_shape=(
            jax.ShapeDtypeStruct((1, 576, 256), BF),
            jax.ShapeDtypeStruct((4, 576, 256), BF),
        ),
        in_specs=[hbm, hbm, vmem, hbm, vmem, vmem],
        out_specs=(vmem, vmem),
        scratch_shapes=[pltpu.VMEM(*spec) for spec in SCRATCH.values()]
        + [pltpu.SemaphoreType.DMA((n,)) for n in SEMS.values()],
        compiler_params=pltpu.CompilerParams(
            collective_id=0, has_side_effects=True, vmem_limit_bytes=56 * 1024 * 1024
        ),
    )(residual, enc_weight, enc_bias, wt, dec_bias, target)
    enc, dec = pl.pallas_call(
        copy_out,
        out_shape=(jax.ShapeDtypeStruct(enc.shape, BF), jax.ShapeDtypeStruct(dec.shape, BF)),
        in_specs=[vmem, vmem],
        out_specs=(hbm, hbm),
        scratch_shapes=[pltpu.SemaphoreType.DMA((2,))],
    )(enc, dec)
    return enc, jnp.swapaxes(dec, 1, 2)[:, None]


def solution(mesh):
    in_specs = (
        P("layer", "dp", None),
        P("layer", None, "feat"),
        P("layer", "feat"),
        P(None, "layer", "feat", "dp"),
        P("layer", "dp"),
        P("layer", "feat", "dp"),
    )
    out_specs = (P("layer", "dp", "feat"), P(None, "layer", "feat", "dp"))
    return jax.shard_map(shards, mesh=mesh, in_specs=in_specs, out_specs=out_specs, check_vma=False)
```

```python
import math

import jax
import jax.numpy as jnp
from jax import lax
from jax.experimental import pallas as pl
from jax.experimental.pallas import tpu as pltpu
from jax.sharding import PartitionSpec as P

MESH = pl.DeviceIdType.MESH
BF = jnp.bfloat16
F32 = jnp.float32
WIN = 640

SEMS = dict(
    load=3, ar=64, az=12, a_n1=16, a_n2=16, a_rl=16,
    rr=4, rr_s=4, rc=3, rc_s=3,
    pc=4, pc_s=4,
    yb=12, yb_s=12, zb=3, zb_s=3,
    cz=3, cz_s=3, cy=12, cy_s=12, cc=4, cc_s=4,
    xr=8, xl=8, xe=8, x_s=24, zc=64, zc_s=16, e=16, e_s=12,
)

SCRATCH = dict(
    resid=((256, 2304), BF), w=((2304, 256), BF), wt=((4, 576, 256), BF),
    pos=((4, 64, 256), F32), codes=((4, 4, 4, 64, 256), BF),
    rw=((4, 256, WIN), BF), rwt=((4, WIN, 256), BF),
    acc=((4, 4, 2, 32, 576), F32), po=((4, 4, 32, 576), BF), pc=((4, 4, 32, 576), BF),
    yst=((12, 32, 576), BF), yb=((12, 32, 576), BF),
    tz=((32, 576), F32), zst=((3, 32, 576), BF), zb=((3, 32, 576), BF),
    g=((4, 4, 2, 32, 576), BF), gt=((4, 576, 256), BF),
    bt=((4, 4, 4, 64, 256), BF), xr=((8, 2, 64, 256), BF), xl=((8, 2, 64, 256), BF), xe=((8, 2, 64, 256), BF),
    s=((8, 2, 64, 256), F32), ss=((16, 64, 256), BF), zc=((4, 16, 64, 256), BF),
    cg=((4, 4, 64, 256), BF), eacc=((WIN, 256), F32),
)


def order(p):
    return jnp.where(p == 0, 0, jnp.where(p == 1, 3, p - 1))


def place(b):
    return jnp.where(b == 0, 0, jnp.where(b == 3, 1, b + 1))


def body(*refs):
    resid_h, w_h, bias, wt_h, dbias, target, enc_o, dec_o = refs[:8]
    R = dict(zip(SCRATCH, refs[8 : 8 + len(SCRATCH)]))
    S = dict(zip(SEMS, refs[8 + len(SCRATCH) :]))
    resid, w, wt, pos, codes = R["resid"], R["w"], R["wt"], R["pos"], R["codes"]
    f = lax.axis_index("feat")
    t = lax.axis_index("layer")
    d = lax.axis_index("dp")
    c, z, y = lax.rem(f, 2), lax.rem(f // 2, 4), f // 8

    def at(yy, zz, core):
        return (lax.rem(yy + 8, 4) * 4 + lax.rem(zz + 8, 4)) * 2 + core

    def along_z(k):
        g = lax.rem(z * 4 + d + k + 16, 16)
        return (at(y, g // 4, c), t, lax.rem(g, 4))

    dev_core = (at(y, z, 1 - c), t, d)
    dev_yp, dev_ym = (at(y + 1, z, c), t, d), (at(y - 1, z, c), t, d)
    dev_zp, dev_zm = (at(y, z + 1, c), t, d), (at(y, z - 1, c), t, d)
    dev_xp, dev_xm = (f, lax.rem(t + 1, 4), d), (f, lax.rem(t + 3, 4), d)
    dev_z2, dev_y2 = (at(y, z + 2, c), t, d), (at(y + 2, z, c), t, d)
    others = [(f, t, lax.rem(d + k, 4)) for k in (1, 2, 3)]
    ym, yp, y2 = lax.rem(y + 3, 4), lax.rem(y + 1, 4), lax.rem(y + 2, 4)
    zm, zp, z2 = lax.rem(z + 3, 4), lax.rem(z + 1, 4), lax.rem(z + 2, 4)
    pd = place(d)

    def copy(src, dst, ssem, rsem, dev):
        return pltpu.make_async_remote_copy(
            src_ref=src, dst_ref=dst, send_sem=ssem, recv_sem=rsem, device_id=dev, device_id_type=MESH
        )

    def arrived(dst, rsem):
        copy(dst, dst, S["load"].at[0], rsem, dev_core).wait_recv()

    def sent(src, ssem):
        copy(src, src, ssem, S["load"].at[0], dev_core).wait_send()

    loads = [
        pltpu.make_async_copy(resid_h.at[0], resid, S["load"].at[0]),
        pltpu.make_async_copy(w_h.at[0], w, S["load"].at[1]),
        pltpu.make_async_copy(wt_h, wt, S["load"].at[2]),
    ]
    for one in loads:
        one.start()

    barrier = pltpu.get_barrier_semaphore()
    partners = [dev_core, dev_yp, dev_ym, dev_zp, dev_zm, dev_xp, dev_xm]
    partners += [dev_y2, dev_z2] + others + [along_z(k) for k in (1, -1, 2, -2)]
    for dev in partners:
        pl.semaphore_signal(barrier, inc=1, device_id=dev, device_id_type=MESH)
    pl.semaphore_wait(barrier, len(partners))

    loads[0].wait()
    loads[1].wait()
    pre = jnp.dot(resid[...], w[...], preferred_element_type=F32) + bias[...]
    positive = jnp.maximum(pre, 0.0)
    pos[...] = positive.reshape(4, 64, 256)
    codes[t, :, pd] = (positive * positive).astype(BF).reshape(4, 64, 256)
    loads[2].wait()

    def chunk_z(i):
        return lax.rem(z + jnp.where(i == 0, 2, jnp.where(i == 1, 1, jnp.where(i == 2, 3, 0))), 4)

    def relays(b):
        side = (b == 0) | (b == 3)
        return ((t == 0) & side) | ((t == 2) & jnp.logical_not(side)) | (t == 3)

    relay_from = jnp.where(t == 3, 0, 1)
    dev_relay = (f, jnp.where(t == 3, 2, 3), d)

    def second(b):
        return (t == 0) | ((t == 1) & ((b == 0) | (b == 3)))

    def to_line(i):
        blk = codes.at[t, chunk_z(i), pd]
        for k, dev in enumerate(others):
            copy(blk, blk, S["az"].at[i * 3 + k], S["ar"].at[t * 16 + i * 4 + pd], dev).start()

    def to_layers(i, b):
        p = place(b)
        n = i * 4 + p
        blk = codes.at[t, chunk_z(i), p]
        sem = S["ar"].at[t * 16 + n]

        @pl.when(t < 3)
        def _():
            copy(blk, blk, S["a_n1"].at[n], sem, dev_xp).start()

        @pl.when(second(b))
        def _():
            copy(blk, blk, S["a_n2"].at[n], sem, dev_xm).start()

    def relay(i, b):
        @pl.when(relays(b))
        def _():
            p = place(b)
            blk = codes.at[relay_from, chunk_z(i), p]
            sem = S["ar"].at[relay_from * 16 + i * 4 + p]
            arrived(blk, sem)
            copy(blk, blk, S["a_rl"].at[i * 4 + p], sem, dev_relay).start()

    rw, rwt = R["rw"], R["rwt"]

    def start_col(k):
        return pl.multiple_of(k * 576 - 64 * lax.rem(k, 2), 128)

    def move_cols(k, lo, size, slot):
        rows = pl.ds(pl.multiple_of(c * 128 + lo, 64), size)
        dev = along_z(k)
        src = resid.at[rows, pl.ds(start_col(dev[2]), WIN)]
        return copy(src, rw.at[pd, rows], S["rr_s"].at[slot], S["rr"].at[slot], dev)

    col_moves = [move_cols(1, 0, 128, 0), move_cols(-1, 0, 128, 1), move_cols(2, 0, 64, 2), move_cols(-2, 64, 64, 3)]
    half = pl.ds(pl.multiple_of(c * 128, 128), 128)
    other_half = pl.ds(pl.multiple_of((1 - c) * 128, 128), 128)
    slots = [place(lax.rem(d + k, 4)) for k in (3, 1, 2)]
    core_moves = [
        copy(rw.at[k, half], rw.at[k, half], S["rc_s"].at[n], S["rc"].at[n], dev_core) for n, k in enumerate(slots)
    ]

    acc, po, pc = R["acc"], R["po"], R["pc"]

    def recon_chunk(i):
        zz = chunk_z(i)

        @pl.loop(0, 12)
        def _(n):
            l, p = n // 4, lax.rem(n, 4)
            relayed = relays(order(p)) & (l == relay_from)

            @pl.when((l < t) & jnp.logical_not(relayed))
            def _():
                arrived(codes.at[l, zz, p], S["ar"].at[l * 16 + i * 4 + p])

        for top in range(4):
            @pl.when(t == top)
            def _():
                total = None
                for l in range(top + 1):
                    term = lax.dot_general(
                        codes[l, zz].reshape(256, 256), wt[l], (((1,), (1,)), ((), ())), preferred_element_type=F32
                    )
                    total = term if total is None else total + term
                acc[i] = total.reshape(4, 2, 32, 576)

        po[i] = acc[i, :, 1 - c].astype(BF)
        copy(po.at[i], pc.at[i], S["pc_s"].at[i], S["pc"].at[i], dev_core).start()

    yst, yb = R["yst"], R["yb"]

    def partial(i, yy):
        p = place(yy)
        return acc[i, p, c] + pc[i, p].astype(F32)

    def y_part(i):
        arrived(pc.at[i], S["pc"].at[i])
        for k, (yy, dev) in enumerate(((yp, dev_yp), (ym, dev_ym), (y2, dev_y2))):
            n = i * 3 + k
            yst[n] = partial(i, yy).astype(BF)
            copy(yst.at[n], yb.at[n], S["yb_s"].at[n], S["yb"].at[n], dev).start()

    tz, zst, zb = R["tz"], R["zst"], R["zb"]

    def z_part(i):
        total = partial(i, y)
        for k in range(3):
            n = i * 3 + k
            arrived(yb.at[n], S["yb"].at[n])
            total = total + yb[n].astype(F32)
        tz[...] = total

        for k, dev in enumerate((dev_z2, dev_zp, dev_zm)):
            @pl.when(i == k)
            def _():
                zst[k] = total.astype(BF)
                copy(zst.at[k], zb.at[k], S["zb_s"].at[k], S["zb"].at[k], dev).start()

    for i in range(4):
        to_line(i)
    for i in range(4):
        to_layers(i, d)

    @pl.loop(0, 8)
    def _(k):
        @pl.when(k < 4)
        def _():
            for h in range(1, 4):
                for b in (d - h, d + h):
                    @pl.when((b >= 0) & (b < 4))
                    def _():
                        p = place(b)
                        arrived(codes.at[t, chunk_z(k), p], S["ar"].at[t * 16 + k * 4 + p])
                        to_layers(k, b)

        @pl.when((k >= 1) & (k < 5))
        def _():
            relay(k - 1, d)
            for h in range(1, 4):
                for b in (d - h, d + h):
                    @pl.when((b >= 0) & (b < 4))
                    def _():
                        relay(k - 1, b)

        @pl.when((k >= 4) & (k < 8))
        def _():
            z_part(k - 4)

        @pl.when((k >= 3) & (k < 7))
        def _():
            y_part(k - 3)

        @pl.when((k >= 2) & (k < 6))
        def _():
            recon_chunk(k - 2)

    scale = 1.0 / math.sqrt(1024)
    g = R["g"]
    py = place(y)
    recon = tz[...]
    for k in range(3):
        arrived(zb.at[k], S["zb"].at[k])
        recon = recon + zb[k].astype(F32)
    g[z, py, c] = ((recon + dbias[...] - target[0].astype(F32)) * scale).astype(BF)

    def block_z(j):
        return lax.rem(z + jnp.where(j == 0, 0, jnp.where(j == 1, 3, jnp.where(j == 2, 1, 2))), 4)

    def to_y(j):
        blk = g.at[block_z(j), py, c]
        for k, dev in enumerate((dev_yp, dev_ym, dev_y2)):
            copy(blk, blk, S["cy_s"].at[j * 3 + k], S["cy"].at[j * 3 + k], dev).start()

    def from_z(j):
        arrived(g.at[block_z(j), py, c], S["cz"].at[j - 1])
        to_y(j)

    def from_y(j):
        for k, yy in enumerate((ym, yp, y2)):
            arrived(g.at[block_z(j), place(yy), c], S["cy"].at[j * 3 + k])
        blk = g.at[block_z(j), :, c]
        copy(blk, blk, S["cc_s"].at[j], S["cc"].at[j], dev_core).start()

    bt, xr, xl, xe, s, ss, zc = R["bt"], R["xr"], R["xl"], R["xe"], R["s"], R["ss"], R["zc"]
    gt, cg, eacc = R["gt"], R["cg"], R["eacc"]

    def x_send(k, u, l, dst, name, dev):
        src = bt.at[l, u // 2, pl.ds(2 * lax.rem(u, 2), 2)]
        copy(src, dst.at[u], S["x_s"].at[k * 8 + u], S[name].at[u], dev).start()

    def back(j):
        zz = block_z(j)

        arrived(g.at[zz, :, 1 - c], S["cc"].at[j])

        @pl.loop(0, t + 1)
        def _(l):
            term = jnp.dot(g[zz].reshape(256, 576), wt[l], preferred_element_type=F32)
            bt[l, j] = term.astype(BF).reshape(4, 64, 256)

        for h in range(2):
            u = j * 2 + h

            @pl.when(t == 1)
            def _():
                x_send(0, u, 0, xr, "xr", dev_xm)

            @pl.when(t == 2)
            def _():
                x_send(0, u, 0, xl, "xl", dev_xp)
                if h == 0:
                    x_send(1, u, 1, xr, "xr", dev_xm)

            @pl.when(t == 3)
            def _():
                x_send(1, u, 1, xe, "xe", dev_xp if h == 0 else dev_xm)
                x_send(2, u, 2, xr, "xr", dev_xm)

    def add_in(l, u, other, name):
        arrived(other.at[u], S[name].at[u])
        j, part = u // 2, pl.ds(2 * lax.rem(u, 2), 2)
        bt[l, j, part] = (bt[l, j, part].astype(F32) + other[u].astype(F32)).astype(BF)

    def x_second(u):
        h = lax.rem(u, 2)

        @pl.when(t == 3)
        def _():
            add_in(0, u, xl, "xl")
            x_send(0, u, 0, xl, "xl", dev_xp)

        @pl.when((t == 2) & (h == 1))
        def _():
            add_in(1, u, xe, "xe")
            x_send(1, u, 1, xr, "xr", dev_xm)

        @pl.when((t == 0) & (h == 0))
        def _():
            arrived(xe.at[u], S["xe"].at[u])
            copy(xe.at[u], xl.at[u], S["x_s"].at[u], S["xl"].at[u], dev_xp).start()

    def x_sum(u):
        h = lax.rem(u, 2)
        s[u] = bt[t, u // 2, pl.ds(2 * h, 2)].astype(F32)

        @pl.when(t < 3)
        def _():
            arrived(xr.at[u], S["xr"].at[u])
            s[u] += xr[u].astype(F32)

        @pl.when((t == 0) | ((t == 1) & (h == 0)))
        def _():
            arrived(xl.at[u], S["xl"].at[u])
            s[u] += xl[u].astype(F32)

        @pl.loop(0, 2)
        def _(r):
            p = 2 * h + r
            n = (u // 2) * 4 + p
            q = order(p)

            @pl.when(q != d)
            def _():
                ss[n] = s[u, r].astype(BF)
                copy(ss.at[n], zc.at[d, n], S["zc_s"].at[n], S["zc"].at[d * 16 + n], (f, t, q)).start()

    def final(u):
        @pl.when(pd // 2 == lax.rem(u, 2))
        def _():
            j = u // 2
            n = j * 4 + pd
            total = s[u, lax.rem(pd, 2)]
            for k in (1, 3, 2):
                q = lax.rem(d + k, 4)
                arrived(zc.at[q, n], S["zc"].at[q * 16 + n])
                total = total + zc[q, n].astype(F32)

            cg[j, pd] = (total * 2.0 * pos[block_z(j)]).astype(BF)
            blk = cg.at[j, pd]
            for k, dev in enumerate(others):
                copy(blk, blk, S["e_s"].at[j * 3 + k], S["e"].at[n], dev).start()

    def gather(u):
        @pl.loop(0, 2)
        def _(r):
            p = 2 * lax.rem(u, 2) + r

            @pl.when(p != pd)
            def _():
                arrived(cg.at[u // 2, p], S["e"].at[(u // 2) * 4 + p])

    def dec_grad(i):
        @pl.when(i <= t)
        def _():
            total = None
            for k in range(4):
                term = jnp.dot(gt[k], codes[i, k].reshape(256, 256), preferred_element_type=F32)
                total = term if total is None else total + term
            dec_o[i] = total.astype(BF)

        @pl.when(i > t)
        def _():
            dec_o[i] = jnp.zeros((576, 256), BF)

    own = g.at[z, py, c]
    for k, dev in enumerate((dev_zp, dev_zm, dev_z2)):
        copy(own, own, S["cz_s"].at[k], S["cz"].at[k], dev).start()
    to_y(0)
    eacc[...] = jnp.zeros_like(eacc)
    from_y(0)
    from_z(1)
    from_z(2)
    back(0)
    from_y(1)
    back(1)
    from_y(2)

    @pl.loop(0, 7)
    def _(k):
        def stage(lag, step):
            @pl.when((k >= lag) & (k < lag + 4))
            def _():
                j = k - lag
                step(2 * j)
                step(2 * j + 1)

        stage(0, x_second)

        @pl.when(k == 0)
        def _():
            back(2)
            from_z(3)
            for one in col_moves:
                one.start()
            rw[pd] = resid[:, pl.ds(start_col(d), WIN)]

        @pl.when(k == 1)
        def _():
            from_y(3)
            back(3)

        @pl.when(k == 2)
        def _():
            for q in range(4):
                gt[q] = g[q].reshape(256, 576).T

        stage(1, x_sum)

        @pl.when((k >= 3) & (k < 5))
        def _():
            dec_grad(2 * k - 6)
            dec_grad(2 * k - 5)

        @pl.when(k == 2)
        def _():
            arrived(rw.at[slots[0], half], S["rr"].at[0])
            arrived(rw.at[slots[1], half], S["rr"].at[1])
            arrived(rw.at[slots[2], pl.ds(pl.multiple_of(c * 128, 64), 64)], S["rr"].at[2])
            arrived(rw.at[slots[2], pl.ds(pl.multiple_of(c * 128 + 64, 64), 64)], S["rr"].at[3])
            for one in core_moves:
                one.start()

        stage(2, final)

        @pl.when(k == 3)
        def _():
            for n, m in enumerate(slots):
                arrived(rw.at[m, other_half], S["rc"].at[n])

            @pl.loop(0, 4)
            def _(j):
                rwt[j] = rw[:, pl.ds(pl.multiple_of(64 * block_z(j), 64), 64)].reshape(256, WIN).T

        stage(3, gather)

        @pl.when(k >= 3)
        def _():
            eacc[...] += jnp.dot(rwt[k - 3], cg[k - 3].reshape(256, 256), preferred_element_type=F32)

    shift = pl.multiple_of(64 * lax.rem(d, 2), 64)
    enc_o[0] = eacc[pl.ds(shift, 576)].astype(BF)

    @pl.loop(0, 16)
    def _(n):
        b = order(lax.rem(n, 4))
        blk = ss.at[n]

        @pl.when(t < 3)
        def _():
            sent(blk, S["a_n1"].at[n])

        @pl.when(second(b))
        def _():
            sent(blk, S["a_n2"].at[n])

        @pl.when(relays(b))
        def _():
            sent(blk, S["a_rl"].at[n])

        @pl.when(d != b)
        def _():
            sent(blk, S["zc_s"].at[n])

    @pl.loop(0, 12)
    def _(n):
        sent(ss.at[0], S["az"].at[n])
        sent(ss.at[0], S["e_s"].at[n])
        sent(own, S["yb_s"].at[n])
        sent(own, S["cy_s"].at[n])

    @pl.loop(0, 8)
    def _(u):
        @pl.when((t > 0) | (lax.rem(u, 2) == 0))
        def _():
            sent(xr.at[u], S["x_s"].at[u])

        @pl.when(t >= 2)
        def _():
            sent(xr.at[u], S["x_s"].at[8 + u])

        @pl.when(t == 3)
        def _():
            sent(xr.at[u], S["x_s"].at[16 + u])

    @pl.loop(0, 4)
    def _(j):
        sent(po.at[j], S["pc_s"].at[j])
        sent(po.at[j], S["cc_s"].at[j])

    for k in range(3):
        sent(own, S["zb_s"].at[k])
        sent(own, S["cz_s"].at[k])
        col_moves[k].wait_send()
        core_moves[k].wait_send()
    col_moves[3].wait_send()


def copy_out(enc, dec, enc_o, dec_o, sems):
    moves = [pltpu.make_async_copy(enc, enc_o, sems.at[0]), pltpu.make_async_copy(dec, dec_o, sems.at[1])]
    for one in moves:
        one.start()
    for one in moves:
        one.wait()


def shards(residual, enc_weight, enc_bias, dec_weight, dec_bias, target):
    wt = jnp.swapaxes(dec_weight[:, 0], 1, 2)
    vmem = pl.BlockSpec(memory_space=pltpu.VMEM)
    hbm = pl.BlockSpec(memory_space=pl.ANY)
    enc, dec = pl.pallas_call(
        body,
        out_shape=(
            jax.ShapeDtypeStruct((1, 576, 256), BF),
            jax.ShapeDtypeStruct((4, 576, 256), BF),
        ),
        in_specs=[hbm, hbm, vmem, hbm, vmem, vmem],
        out_specs=(vmem, vmem),
        scratch_shapes=[pltpu.VMEM(*spec) for spec in SCRATCH.values()]
        + [pltpu.SemaphoreType.DMA((n,)) for n in SEMS.values()],
        compiler_params=pltpu.CompilerParams(
            collective_id=0, has_side_effects=True, vmem_limit_bytes=56 * 1024 * 1024
        ),
    )(residual, enc_weight, enc_bias, wt, dec_bias, target)
    enc, dec = pl.pallas_call(
        copy_out,
        out_shape=(jax.ShapeDtypeStruct(enc.shape, BF), jax.ShapeDtypeStruct(dec.shape, BF)),
        in_specs=[vmem, vmem],
        out_specs=(hbm, hbm),
        scratch_shapes=[pltpu.SemaphoreType.DMA((2,))],
    )(enc, dec)
    return enc, jnp.swapaxes(dec, 1, 2)[:, None]


def solution(mesh):
    in_specs = (
        P("layer", "dp", None),
        P("layer", None, "feat"),
        P("layer", "feat"),
        P(None, "layer", "feat", "dp"),
        P("layer", "dp"),
        P("layer", "feat", "dp"),
    )
    out_specs = (P("layer", "dp", "feat"), P(None, "layer", "feat", "dp"))
    return jax.shard_map(shards, mesh=mesh, in_specs=in_specs, out_specs=out_specs, check_vma=False)
```

```python
import math

import jax
import jax.numpy as jnp
from jax import lax
from jax.experimental import pallas as pl
from jax.experimental.pallas import tpu as pltpu
from jax.sharding import PartitionSpec as P

MESH = pl.DeviceIdType.MESH
BF = jnp.bfloat16
F32 = jnp.float32
WIN = 640

SEMS = dict(
    load=3, ar=64, az=12, a_n1=16, a_n2=16, a_rl=16,
    rr=4, rr_s=4, rc=3, rc_s=3,
    pc=4, pc_s=4,
    yb=12, yb_s=12, zb=3, zb_s=3,
    cz=3, cz_s=3, cy=12, cy_s=12, cc=4, cc_s=4,
    xr=8, xl=8, xe=8, x_s=24, zc=64, zc_s=16, e=16, e_s=12,
)

SCRATCH = dict(
    resid=((256, 2304), BF), w=((2304, 256), BF), wt=((4, 576, 256), BF),
    pos=((4, 64, 256), F32), codes=((4, 4, 4, 64, 256), BF),
    rw=((4, 256, WIN), BF), rwt=((4, WIN, 256), BF),
    acc=((4, 4, 2, 32, 576), F32), po=((4, 4, 32, 576), BF), pc=((4, 4, 32, 576), BF),
    yst=((12, 32, 576), BF), yb=((12, 32, 576), BF),
    tz=((32, 576), F32), zst=((3, 32, 576), BF), zb=((3, 32, 576), BF),
    g=((4, 4, 2, 32, 576), BF), gt=((4, 576, 256), BF),
    bt=((4, 4, 4, 64, 256), BF), xr=((8, 2, 64, 256), BF), xl=((8, 2, 64, 256), BF), xe=((8, 2, 64, 256), BF),
    s=((8, 2, 64, 256), F32), ss=((16, 64, 256), BF), zc=((4, 16, 64, 256), BF),
    cg=((4, 4, 64, 256), BF), eacc=((WIN, 256), F32),
)


def order(p):
    return jnp.where(p == 0, 0, jnp.where(p == 1, 3, p - 1))


def place(b):
    return jnp.where(b == 0, 0, jnp.where(b == 3, 1, b + 1))


def body(*refs):
    resid_h, w_h, bias, wt_h, dbias, target, enc_o, dec_o = refs[:8]
    R = dict(zip(SCRATCH, refs[8 : 8 + len(SCRATCH)]))
    S = dict(zip(SEMS, refs[8 + len(SCRATCH) :]))
    resid, w, wt, pos, codes = R["resid"], R["w"], R["wt"], R["pos"], R["codes"]
    f = lax.axis_index("feat")
    t = lax.axis_index("layer")
    d = lax.axis_index("dp")
    c, z, y = lax.rem(f, 2), lax.rem(f // 2, 4), f // 8

    def at(yy, zz, core):
        return (lax.rem(yy + 8, 4) * 4 + lax.rem(zz + 8, 4)) * 2 + core

    def along_z(k):
        g = lax.rem(z * 4 + d + k + 16, 16)
        return (at(y, g // 4, c), t, lax.rem(g, 4))

    dev_core = (at(y, z, 1 - c), t, d)
    dev_yp, dev_ym = (at(y + 1, z, c), t, d), (at(y - 1, z, c), t, d)
    dev_zp, dev_zm = (at(y, z + 1, c), t, d), (at(y, z - 1, c), t, d)
    dev_xp, dev_xm = (f, lax.rem(t + 1, 4), d), (f, lax.rem(t + 3, 4), d)
    dev_z2, dev_y2 = (at(y, z + 2, c), t, d), (at(y + 2, z, c), t, d)
    others = [(f, t, lax.rem(d + k, 4)) for k in (1, 2, 3)]
    ym, yp, y2 = lax.rem(y + 3, 4), lax.rem(y + 1, 4), lax.rem(y + 2, 4)
    zm, zp, z2 = lax.rem(z + 3, 4), lax.rem(z + 1, 4), lax.rem(z + 2, 4)
    pd = place(d)

    def copy(src, dst, ssem, rsem, dev):
        return pltpu.make_async_remote_copy(
            src_ref=src, dst_ref=dst, send_sem=ssem, recv_sem=rsem, device_id=dev, device_id_type=MESH
        )

    def arrived(dst, rsem):
        copy(dst, dst, S["load"].at[0], rsem, dev_core).wait_recv()

    def sent(src, ssem):
        copy(src, src, ssem, S["load"].at[0], dev_core).wait_send()

    loads = [
        pltpu.make_async_copy(resid_h.at[0], resid, S["load"].at[0]),
        pltpu.make_async_copy(w_h.at[0], w, S["load"].at[1]),
        pltpu.make_async_copy(wt_h, wt, S["load"].at[2]),
    ]
    for one in loads:
        one.start()

    barrier = pltpu.get_barrier_semaphore()
    partners = [dev_core, dev_yp, dev_ym, dev_zp, dev_zm, dev_xp, dev_xm]
    partners += [dev_y2, dev_z2] + others + [along_z(k) for k in (1, -1, 2, -2)]
    for dev in partners:
        pl.semaphore_signal(barrier, inc=1, device_id=dev, device_id_type=MESH)
    pl.semaphore_wait(barrier, len(partners))

    loads[0].wait()
    loads[1].wait()
    pre = jnp.dot(resid[...], w[...], preferred_element_type=F32) + bias[...]
    positive = jnp.maximum(pre, 0.0)
    pos[...] = positive.reshape(4, 64, 256)
    codes[t, :, pd] = (positive * positive).astype(BF).reshape(4, 64, 256)

    def chunk_z(i):
        return lax.rem(z + jnp.where(i == 0, 2, jnp.where(i == 1, 1, jnp.where(i == 2, 3, 0))), 4)

    def relays(b):
        side = (b == 0) | (b == 3)
        return ((t == 0) & side) | ((t == 2) & jnp.logical_not(side)) | (t == 3)

    relay_from = jnp.where(t == 3, 0, 1)
    dev_relay = (f, jnp.where(t == 3, 2, 3), d)

    def second(b):
        return (t == 0) | ((t == 1) & ((b == 0) | (b == 3)))

    def to_line(i):
        blk = codes.at[t, chunk_z(i), pd]
        for k, dev in enumerate(others):
            copy(blk, blk, S["az"].at[i * 3 + k], S["ar"].at[t * 16 + i * 4 + pd], dev).start()

    def to_layers(i, b):
        p = place(b)
        n = i * 4 + p
        blk = codes.at[t, chunk_z(i), p]
        sem = S["ar"].at[t * 16 + n]

        @pl.when(t < 3)
        def _():
            copy(blk, blk, S["a_n1"].at[n], sem, dev_xp).start()

        @pl.when(second(b))
        def _():
            copy(blk, blk, S["a_n2"].at[n], sem, dev_xm).start()

    def relay(i, b):
        @pl.when(relays(b))
        def _():
            p = place(b)
            blk = codes.at[relay_from, chunk_z(i), p]
            sem = S["ar"].at[relay_from * 16 + i * 4 + p]
            arrived(blk, sem)
            copy(blk, blk, S["a_rl"].at[i * 4 + p], sem, dev_relay).start()

    rw, rwt = R["rw"], R["rwt"]

    def start_col(k):
        return pl.multiple_of(k * 576 - 64 * lax.rem(k, 2), 128)

    def move_cols(k, lo, size, slot):
        rows = pl.ds(pl.multiple_of(c * 128 + lo, 64), size)
        dev = along_z(k)
        src = resid.at[rows, pl.ds(start_col(dev[2]), WIN)]
        return copy(src, rw.at[pd, rows], S["rr_s"].at[slot], S["rr"].at[slot], dev)

    col_moves = [move_cols(1, 0, 128, 0), move_cols(-1, 0, 128, 1), move_cols(2, 0, 64, 2), move_cols(-2, 64, 64, 3)]
    half = pl.ds(pl.multiple_of(c * 128, 128), 128)
    other_half = pl.ds(pl.multiple_of((1 - c) * 128, 128), 128)
    slots = [place(lax.rem(d + k, 4)) for k in (3, 1, 2)]
    core_moves = [
        copy(rw.at[k, half], rw.at[k, half], S["rc_s"].at[n], S["rc"].at[n], dev_core) for n, k in enumerate(slots)
    ]

    acc, po, pc = R["acc"], R["po"], R["pc"]

    def recon_chunk(i):
        zz = chunk_z(i)

        @pl.loop(0, 12)
        def _(n):
            l, p = n // 4, lax.rem(n, 4)
            relayed = relays(order(p)) & (l == relay_from)

            @pl.when((l < t) & jnp.logical_not(relayed))
            def _():
                arrived(codes.at[l, zz, p], S["ar"].at[l * 16 + i * 4 + p])

        for top in range(4):
            @pl.when(t == top)
            def _():
                total = None
                for l in range(top + 1):
                    term = lax.dot_general(
                        codes[l, zz].reshape(256, 256), wt[l], (((1,), (1,)), ((), ())), preferred_element_type=F32
                    )
                    total = term if total is None else total + term
                acc[i] = total.reshape(4, 2, 32, 576)

        po[i] = acc[i, :, 1 - c].astype(BF)
        copy(po.at[i], pc.at[i], S["pc_s"].at[i], S["pc"].at[i], dev_core).start()

    yst, yb = R["yst"], R["yb"]

    def partial(i, yy):
        p = place(yy)
        return acc[i, p, c] + pc[i, p].astype(F32)

    def y_part(i):
        arrived(pc.at[i], S["pc"].at[i])
        for k, (yy, dev) in enumerate(((yp, dev_yp), (ym, dev_ym), (y2, dev_y2))):
            n = i * 3 + k
            yst[n] = partial(i, yy).astype(BF)
            copy(yst.at[n], yb.at[n], S["yb_s"].at[n], S["yb"].at[n], dev).start()

    tz, zst, zb = R["tz"], R["zst"], R["zb"]

    def z_part(i):
        total = partial(i, y)
        for k in range(3):
            n = i * 3 + k
            arrived(yb.at[n], S["yb"].at[n])
            total = total + yb[n].astype(F32)
        tz[...] = total

        for k, dev in enumerate((dev_z2, dev_zp, dev_zm)):
            @pl.when(i == k)
            def _():
                zst[k] = total.astype(BF)
                copy(zst.at[k], zb.at[k], S["zb_s"].at[k], S["zb"].at[k], dev).start()

    for i in range(4):
        to_layers(i, d)
        to_line(i)
    loads[2].wait()

    @pl.loop(0, 8)
    def _(k):
        @pl.when(k < 4)
        def _():
            for h in range(1, 4):
                for b in (d - h, d + h):
                    @pl.when((b >= 0) & (b < 4))
                    def _():
                        p = place(b)
                        arrived(codes.at[t, chunk_z(k), p], S["ar"].at[t * 16 + k * 4 + p])
                        to_layers(k, b)

        @pl.when((k >= 1) & (k < 5))
        def _():
            relay(k - 1, d)
            for h in range(1, 4):
                for b in (d - h, d + h):
                    @pl.when((b >= 0) & (b < 4))
                    def _():
                        relay(k - 1, b)

        @pl.when((k >= 4) & (k < 8))
        def _():
            z_part(k - 4)

        @pl.when((k >= 3) & (k < 7))
        def _():
            y_part(k - 3)

        @pl.when((k >= 2) & (k < 6))
        def _():
            recon_chunk(k - 2)

    scale = 1.0 / math.sqrt(1024)
    g = R["g"]
    py = place(y)
    recon = tz[...]
    for k in range(3):
        arrived(zb.at[k], S["zb"].at[k])
        recon = recon + zb[k].astype(F32)
    g[z, py, c] = ((recon + dbias[...] - target[0].astype(F32)) * scale).astype(BF)

    def block_z(j):
        return lax.rem(z + jnp.where(j == 0, 0, jnp.where(j == 1, 3, jnp.where(j == 2, 1, 2))), 4)

    def to_y(j):
        blk = g.at[block_z(j), py, c]
        for k, dev in enumerate((dev_yp, dev_ym, dev_y2)):
            copy(blk, blk, S["cy_s"].at[j * 3 + k], S["cy"].at[j * 3 + k], dev).start()

    def from_z(j):
        arrived(g.at[block_z(j), py, c], S["cz"].at[j - 1])
        to_y(j)

    def from_y(j):
        for k, yy in enumerate((ym, yp, y2)):
            arrived(g.at[block_z(j), place(yy), c], S["cy"].at[j * 3 + k])
        blk = g.at[block_z(j), :, c]
        copy(blk, blk, S["cc_s"].at[j], S["cc"].at[j], dev_core).start()

    bt, xr, xl, xe, s, ss, zc = R["bt"], R["xr"], R["xl"], R["xe"], R["s"], R["ss"], R["zc"]
    gt, cg, eacc = R["gt"], R["cg"], R["eacc"]

    def x_send(k, u, l, dst, name, dev):
        src = bt.at[l, u // 2, pl.ds(2 * lax.rem(u, 2), 2)]
        copy(src, dst.at[u], S["x_s"].at[k * 8 + u], S[name].at[u], dev).start()

    def back(j):
        zz = block_z(j)

        arrived(g.at[zz, :, 1 - c], S["cc"].at[j])

        @pl.loop(0, t + 1)
        def _(l):
            term = jnp.dot(g[zz].reshape(256, 576), wt[l], preferred_element_type=F32)
            bt[l, j] = term.astype(BF).reshape(4, 64, 256)

        for h in range(2):
            u = j * 2 + h

            @pl.when(t == 1)
            def _():
                x_send(0, u, 0, xr, "xr", dev_xm)

            @pl.when(t == 2)
            def _():
                x_send(0, u, 0, xl, "xl", dev_xp)
                if h == 0:
                    x_send(1, u, 1, xr, "xr", dev_xm)

            @pl.when(t == 3)
            def _():
                x_send(1, u, 1, xe, "xe", dev_xp if h == 0 else dev_xm)
                x_send(2, u, 2, xr, "xr", dev_xm)

    def add_in(l, u, other, name):
        arrived(other.at[u], S[name].at[u])
        j, part = u // 2, pl.ds(2 * lax.rem(u, 2), 2)
        bt[l, j, part] = (bt[l, j, part].astype(F32) + other[u].astype(F32)).astype(BF)

    def x_second(u):
        h = lax.rem(u, 2)

        @pl.when(t == 3)
        def _():
            add_in(0, u, xl, "xl")
            x_send(0, u, 0, xl, "xl", dev_xp)

        @pl.when((t == 2) & (h == 1))
        def _():
            add_in(1, u, xe, "xe")
            x_send(1, u, 1, xr, "xr", dev_xm)

        @pl.when((t == 0) & (h == 0))
        def _():
            arrived(xe.at[u], S["xe"].at[u])
            copy(xe.at[u], xl.at[u], S["x_s"].at[u], S["xl"].at[u], dev_xp).start()

    def x_sum(u):
        h = lax.rem(u, 2)
        s[u] = bt[t, u // 2, pl.ds(2 * h, 2)].astype(F32)

        @pl.when(t < 3)
        def _():
            arrived(xr.at[u], S["xr"].at[u])
            s[u] += xr[u].astype(F32)

        @pl.when((t == 0) | ((t == 1) & (h == 0)))
        def _():
            arrived(xl.at[u], S["xl"].at[u])
            s[u] += xl[u].astype(F32)

        @pl.loop(0, 2)
        def _(r):
            p = 2 * h + r
            n = (u // 2) * 4 + p
            q = order(p)

            @pl.when(q != d)
            def _():
                ss[n] = s[u, r].astype(BF)
                copy(ss.at[n], zc.at[d, n], S["zc_s"].at[n], S["zc"].at[d * 16 + n], (f, t, q)).start()

    def final(u):
        @pl.when(pd // 2 == lax.rem(u, 2))
        def _():
            j = u // 2
            n = j * 4 + pd
            total = s[u, lax.rem(pd, 2)]
            for k in (1, 3, 2):
                q = lax.rem(d + k, 4)
                arrived(zc.at[q, n], S["zc"].at[q * 16 + n])
                total = total + zc[q, n].astype(F32)

            cg[j, pd] = (total * 2.0 * pos[block_z(j)]).astype(BF)
            blk = cg.at[j, pd]
            for k, dev in enumerate(others):
                copy(blk, blk, S["e_s"].at[j * 3 + k], S["e"].at[n], dev).start()

    def gather(u):
        @pl.loop(0, 2)
        def _(r):
            p = 2 * lax.rem(u, 2) + r

            @pl.when(p != pd)
            def _():
                arrived(cg.at[u // 2, p], S["e"].at[(u // 2) * 4 + p])

    def dec_grad(i):
        @pl.when(i <= t)
        def _():
            total = None
            for k in range(4):
                term = jnp.dot(gt[k], codes[i, k].reshape(256, 256), preferred_element_type=F32)
                total = term if total is None else total + term
            dec_o[i] = total.astype(BF)

        @pl.when(i > t)
        def _():
            dec_o[i] = jnp.zeros((576, 256), BF)

    own = g.at[z, py, c]
    for k, dev in enumerate((dev_zp, dev_zm, dev_z2)):
        copy(own, own, S["cz_s"].at[k], S["cz"].at[k], dev).start()
    to_y(0)
    eacc[...] = jnp.zeros_like(eacc)
    from_y(0)
    from_z(1)
    from_z(2)
    back(0)
    from_y(1)
    back(1)
    from_y(2)

    @pl.loop(0, 7)
    def _(k):
        def stage(lag, step):
            @pl.when((k >= lag) & (k < lag + 4))
            def _():
                j = k - lag
                step(2 * j)
                step(2 * j + 1)

        stage(0, x_second)

        @pl.when(k == 0)
        def _():
            back(2)
            from_z(3)
            for one in col_moves:
                one.start()
            rw[pd] = resid[:, pl.ds(start_col(d), WIN)]

        @pl.when(k == 1)
        def _():
            from_y(3)
            back(3)

        @pl.when(k == 2)
        def _():
            for q in range(4):
                gt[q] = g[q].reshape(256, 576).T

        stage(1, x_sum)

        @pl.when((k >= 3) & (k < 5))
        def _():
            dec_grad(2 * k - 6)
            dec_grad(2 * k - 5)

        @pl.when(k == 2)
        def _():
            arrived(rw.at[slots[0], half], S["rr"].at[0])
            arrived(rw.at[slots[1], half], S["rr"].at[1])
            arrived(rw.at[slots[2], pl.ds(pl.multiple_of(c * 128, 64), 64)], S["rr"].at[2])
            arrived(rw.at[slots[2], pl.ds(pl.multiple_of(c * 128 + 64, 64), 64)], S["rr"].at[3])
            for one in core_moves:
                one.start()

        stage(2, final)

        @pl.when(k == 3)
        def _():
            for n, m in enumerate(slots):
                arrived(rw.at[m, other_half], S["rc"].at[n])

            @pl.loop(0, 4)
            def _(j):
                rwt[j] = rw[:, pl.ds(pl.multiple_of(64 * block_z(j), 64), 64)].reshape(256, WIN).T

        stage(3, gather)

        @pl.when(k >= 3)
        def _():
            eacc[...] += jnp.dot(rwt[k - 3], cg[k - 3].reshape(256, 256), preferred_element_type=F32)

    shift = pl.multiple_of(64 * lax.rem(d, 2), 64)
    enc_o[0] = eacc[pl.ds(shift, 576)].astype(BF)

    @pl.loop(0, 16)
    def _(n):
        b = order(lax.rem(n, 4))
        blk = ss.at[n]

        @pl.when(t < 3)
        def _():
            sent(blk, S["a_n1"].at[n])

        @pl.when(second(b))
        def _():
            sent(blk, S["a_n2"].at[n])

        @pl.when(relays(b))
        def _():
            sent(blk, S["a_rl"].at[n])

        @pl.when(d != b)
        def _():
            sent(blk, S["zc_s"].at[n])

    @pl.loop(0, 12)
    def _(n):
        sent(ss.at[0], S["az"].at[n])
        sent(ss.at[0], S["e_s"].at[n])
        sent(own, S["yb_s"].at[n])
        sent(own, S["cy_s"].at[n])

    @pl.loop(0, 8)
    def _(u):
        @pl.when((t > 0) | (lax.rem(u, 2) == 0))
        def _():
            sent(xr.at[u], S["x_s"].at[u])

        @pl.when(t >= 2)
        def _():
            sent(xr.at[u], S["x_s"].at[8 + u])

        @pl.when(t == 3)
        def _():
            sent(xr.at[u], S["x_s"].at[16 + u])

    @pl.loop(0, 4)
    def _(j):
        sent(po.at[j], S["pc_s"].at[j])
        sent(po.at[j], S["cc_s"].at[j])

    for k in range(3):
        sent(own, S["zb_s"].at[k])
        sent(own, S["cz_s"].at[k])
        col_moves[k].wait_send()
        core_moves[k].wait_send()
    col_moves[3].wait_send()


def copy_out(enc, dec, enc_o, dec_o, sems):
    moves = [pltpu.make_async_copy(enc, enc_o, sems.at[0]), pltpu.make_async_copy(dec, dec_o, sems.at[1])]
    for one in moves:
        one.start()
    for one in moves:
        one.wait()


def shards(residual, enc_weight, enc_bias, dec_weight, dec_bias, target):
    wt = jnp.swapaxes(dec_weight[:, 0], 1, 2)
    vmem = pl.BlockSpec(memory_space=pltpu.VMEM)
    hbm = pl.BlockSpec(memory_space=pl.ANY)
    enc, dec = pl.pallas_call(
        body,
        out_shape=(
            jax.ShapeDtypeStruct((1, 576, 256), BF),
            jax.ShapeDtypeStruct((4, 576, 256), BF),
        ),
        in_specs=[hbm, hbm, vmem, hbm, vmem, vmem],
        out_specs=(vmem, vmem),
        scratch_shapes=[pltpu.VMEM(*spec) for spec in SCRATCH.values()]
        + [pltpu.SemaphoreType.DMA((n,)) for n in SEMS.values()],
        compiler_params=pltpu.CompilerParams(
            collective_id=0, has_side_effects=True, vmem_limit_bytes=56 * 1024 * 1024
        ),
    )(residual, enc_weight, enc_bias, wt, dec_bias, target)
    enc, dec = pl.pallas_call(
        copy_out,
        out_shape=(jax.ShapeDtypeStruct(enc.shape, BF), jax.ShapeDtypeStruct(dec.shape, BF)),
        in_specs=[vmem, vmem],
        out_specs=(hbm, hbm),
        scratch_shapes=[pltpu.SemaphoreType.DMA((2,))],
    )(enc, dec)
    return enc, jnp.swapaxes(dec, 1, 2)[:, None]


def solution(mesh):
    in_specs = (
        P("layer", "dp", None),
        P("layer", None, "feat"),
        P("layer", "feat"),
        P(None, "layer", "feat", "dp"),
        P("layer", "dp"),
        P("layer", "feat", "dp"),
    )
    out_specs = (P("layer", "dp", "feat"), P(None, "layer", "feat", "dp"))
    return jax.shard_map(shards, mesh=mesh, in_specs=in_specs, out_specs=out_specs, check_vma=False)
```
